128 devices in a mesh: side: 2 (over core), dev: 64 (over z, y, x).
Axes of the slice: x: 4, y: 4, z: 4, core: 2. Of those that a mesh axis runs over, the one named last changes fastest.
Arguments:
- tokens: bfloat16 [512, 7168], P(('side', 'dev')), may hold values from -6 to 6
- routes: int32 [512, 8], P(('side', 'dev')), may hold values from 0 to 15, all different within a row; in each aligned block of 4 rows (0 to 3, 4 to 7, ...) at most 3 rows name the same one
- gates: float32 [512, 8], P(('side', 'dev')), may hold values from 0.05 to 0.6
- w_gate: bfloat16 [128, 7168, 256], P(('side', 'dev')), may hold values from -0.0625 to 0.0625
- w_up: bfloat16 [128, 7168, 256], P(('side', 'dev')), may hold values from -0.0625 to 0.0625
- w_down: bfloat16 [128, 256, 7168], P(('side', 'dev')), may hold values from -0.125 to 0.125
- queries: bfloat16 [512, 128, 576], P(('side', 'dev')), may hold values from -30 to 30
- cache: bfloat16 [512, 1024, 576], P(('side', 'dev')), may hold values from -5 to 5
- lengths: int32 [512], P(('side', 'dev')), may hold values from 2 to 1024, as said below
Outputs:
- moe_out: bfloat16 [512, 7168], P(('side', 'dev'))
- attention_out: bfloat16 [512, 128, 512], P(('side', 'dev'))
The draws below stay inside these ranges and needn't reach their ends.
Inputs may be any that keep to these rules, and one draw needn't show every extreme that they name: `routes`: within each aligned block of 4 tokens (the rows of one device) no expert is named by more than 3 rows, a bound that some block reaches. `lengths`: some request has exactly 1024 valid positions.
All inputs are finite; a program needn't handle non-finite values.
Results may differ from the reference program's by a relative error of at most 0.0057.
Values may be sent and summed in bfloat16 or wider, within the bound.
A program may use at most 128 MiB of HBM per device.

```python
import math
import jax
import jax.numpy as jnp
import numpy as np
from jax import lax

D = 7168
FF = 2048
HEADS = 128
LATENT = 512
ROPE = 64
NOPE = 128
TOP = 8
EXPERTS = 16
REQ_DEV = 4
MAX_LEN = 1024
CAP = 3
SLICES = 8
UNITS = 256
TOKENS = 512
REQUESTS = 512
N_SIDE = 2
N_DEV = 64


def anchor_rows(key):
    base = jax.random.normal(jax.random.fold_in(key, 1), (REQUESTS, LATENT + ROPE), jnp.float32)
    return jnp.clip(base, -4.0, 4.0)


def draw_cache(key, part):
    anchor = anchor_rows(key)
    key = jax.random.fold_in(key, 3)
    first = jax.random.fold_in(key, 0)
    base = jnp.clip(jax.random.normal(first, (REQUESTS, MAX_LEN, LATENT + ROPE), jnp.float32), -5.0, 5.0)
    base = base.at[:, 0, :].set(anchor)
    return base.astype(jnp.bfloat16)


def draw_queries(key, part):
    key = jax.random.fold_in(key, 5)
    first = jax.random.fold_in(key, 0)
    base = jnp.clip(jax.random.normal(first, (REQUESTS, HEADS, LATENT + ROPE), jnp.float32), -5.0, 5.0)
    return base.astype(jnp.bfloat16)


def draw_lengths(key, part):
    key = jax.random.fold_in(key, 7)
    first, second = jax.random.split(key)
    drawn = jax.random.randint(first, (REQUESTS,), 2, MAX_LEN + 1, jnp.int32)
    longest = jax.random.randint(second, (), 0, REQUESTS, jnp.int32)
    return jnp.where(jnp.arange(REQUESTS, dtype=jnp.int32) == longest, MAX_LEN, drawn).astype(jnp.int32)


def level_of(stream_key, dims, cuts, low, top_value):
    def one(position, shards_of):
        draws = jax.random.uniform(jax.random.fold_in(jax.random.fold_in(stream_key, 6), position), (shards_of,), jnp.float32, low / len(cuts), top_value / len(cuts))
        return jnp.repeat(jnp.exp(draws), dims[position] // shards_of).reshape((-1,) + (1,) * (len(dims) - position - 1))

    level = one(*cuts[0])
    for cut in cuts[1:]:
        level = level * one(*cut)
    return level


def shared_out(rng, own, number, rows, amount, top, reach, lean):
    ranking = jax.random.permutation(rng, amount)
    packed, ordinary = shares(amount, rows * top, reach, lean, True), shares(amount, rows * top, reach, lean, False)
    places = jnp.arange(amount)

    def named(sizes, offset_by):
        used = int((sizes > 0).sum())
        fixed = max(1, used // 4)
        passed = fixed + (places - fixed + offset_by * (used - fixed)) % max(1, amount - fixed)
        return jnp.zeros((amount,), jnp.int32).at[ranking[jnp.where(places < fixed, places, passed)]].set(jnp.asarray(sizes, jnp.int32))

    sizes = jnp.where(number % 4 == 0, named(packed, number // 4), named(ordinary, number - number // 4 - 1))
    mixed = jax.random.permutation(jax.random.fold_in(own, 3), amount)
    source_of, taker = mixed[0:amount // 2 * 2:2], mixed[1:amount // 2 * 2:2]
    margin = jnp.minimum(sizes[source_of] - 1, reach - sizes[taker]) // 2
    margin = jnp.where((source_of == ranking[0]) | (taker == ranking[0]) | (sizes[taker] == 0), 0, jnp.maximum(margin, 0))
    passed = jax.random.randint(jax.random.fold_in(own, 4), (amount // 2,), 0, 1 << 20) % (margin + 1)
    sizes = sizes.at[source_of].add(-passed).at[taker].add(passed)
    labels = jnp.searchsorted(jnp.cumsum(sizes), jnp.arange(rows * top), side="right").astype(jnp.int32)
    table = labels.reshape(top, rows).T
    table = table[jax.random.permutation(jax.random.fold_in(own, 1), rows)]
    offset_by = jax.random.randint(jax.random.fold_in(own, 2), (rows, 1), 0, top)
    return jnp.take_along_axis(table, (jnp.arange(top)[None, :] + offset_by) % top, axis=1)


def shares(amount, total, most, lean, full):
    weights = [(1 << 20) // math.isqrt(standing ** lean) + 1 for standing in range(1, amount + 1)]
    largest = most if full else min(most, max(-(-total // amount), total * weights[0] // sum(weights)))
    least = 1 if total - largest >= amount - 1 else 0
    counts, spare = [largest] + [least] * (amount - 1), total - largest - least * (amount - 1)
    while spare > 0:
        movable = [i for i in range(1, amount) if counts[i] < largest] or [i for i in range(1, amount) if counts[i] < most]
        pool, budget = sum([weights[i] for i in movable]), spare
        for i in movable:
            more = min(most - counts[i], max(1, budget * weights[i] // pool), spare)
            counts[i] = counts[i] + more
            spare = spare - more
    return np.array(counts)


def centred(own_key, extent, spread, bound, pieces=(), kind=jnp.bfloat16):
    values = spread * jax.random.normal(own_key, extent, jnp.float32)
    if pieces:
        values = values * level_of(own_key, extent, pieces, -0.22, 0.18)
    return jnp.clip(values, -bound, bound).astype(kind)


def setup_inputs(seed: int = 0) -> dict:
    seeds = jax.random.split(jax.random.key(seed), 10)
    tokens = centred(seeds[0], (TOKENS, D), 1.0, 6.0, ((0, 128),))
    routes_keys = jax.random.split(jax.random.fold_in(seeds[1], 1), TOKENS // REQ_DEV)
    routes_turns = jax.random.permutation(jax.random.fold_in(seeds[1], 3), TOKENS // REQ_DEV)
    routes = jax.vmap(lambda own, number: shared_out(jax.random.fold_in(seeds[1], 2), own, number, REQ_DEV, EXPERTS, TOP, CAP, 1))(routes_keys, routes_turns).reshape((TOKENS, TOP))
    gates = jnp.clip(0.05 + 0.55 * jax.random.uniform(seeds[2], (TOKENS, TOP), jnp.float32) ** level_of(seeds[2], (TOKENS, TOP), ((0, 128),), -0.2, 0.2), 0.05, 0.6)
    w_gate = centred(seeds[3], (EXPERTS * SLICES, D, UNITS), D ** -0.5, 0.0625, ((0, 128),))
    w_up = centred(seeds[4], (EXPERTS * SLICES, D, UNITS), D ** -0.5, 0.0625, ((0, 128),))
    w_down = centred(seeds[5], (EXPERTS * SLICES, UNITS, D), FF ** -0.5, 0.125, ((0, 128),))
    queries = draw_queries(jax.random.fold_in(seeds[9], 71), 0)
    cache = draw_cache(jax.random.fold_in(seeds[9], 71), 0)
    lengths = draw_lengths(jax.random.fold_in(seeds[9], 71), 0)
    return dict(tokens=tokens, routes=routes, gates=gates, w_gate=w_gate, w_up=w_up, w_down=w_down, queries=queries, cache=cache, lengths=lengths)


def attend(block):
    query, keys, length = block
    scale = (NOPE + ROPE) ** -0.5
    scores = jnp.einsum("rhk,rlk->rhl", query.astype(jnp.float32), keys.astype(jnp.float32)) * scale
    valid = jnp.arange(keys.shape[1], dtype=jnp.int32)[None, None, :] < length[:, None, None]
    scores = jnp.where(valid, scores, -1e30)
    highest = jnp.max(scores, -1, keepdims=True)
    weights = jnp.where(valid, jnp.exp(scores - highest), 0.0)
    probabilities = (weights / jnp.sum(weights, -1, keepdims=True)).astype(jnp.bfloat16)
    probabilities = lax.optimization_barrier(probabilities)
    values = keys[:, :, :LATENT].astype(jnp.float32)
    return jnp.einsum("rhl,rlk->rhk", probabilities.astype(jnp.float32), values).astype(jnp.bfloat16)


def reference(tokens, routes, gates, w_gate, w_up, w_down, queries, cache, lengths):
    slices = SLICES
    units = UNITS
    limit = N_SIDE * N_DEV * CAP

    def one_expert(total, expert):
        hits = routes == expert
        chosen = jnp.any(hits, 1)
        weight = jnp.sum(jnp.where(hits, gates, 0.0), 1)
        counted = jnp.sum(chosen.astype(jnp.int32))
        picked = jnp.nonzero(chosen, size=limit, fill_value=0)[0].astype(jnp.int32)
        rows = tokens[picked]
        start = (expert * slices).astype(jnp.int32)
        gate_w = jnp.transpose(lax.dynamic_slice_in_dim(w_gate, start, slices, 0), (1, 0, 2)).reshape(D, FF)
        up_w = jnp.transpose(lax.dynamic_slice_in_dim(w_up, start, slices, 0), (1, 0, 2)).reshape(D, FF)
        down_w = lax.dynamic_slice_in_dim(w_down, start, slices, 0)
        gate = jnp.dot(rows, gate_w, preferred_element_type=jnp.float32)
        upper = jnp.dot(rows, up_w, preferred_element_type=jnp.float32)
        hidden = (jax.nn.silu(gate) * upper).astype(jnp.bfloat16)
        summed = jnp.zeros((limit, D), jnp.float32)
        for piece in range(slices):
            partial_value = jnp.dot(hidden[:, piece * units:(piece + 1) * units], down_w[piece],
                              preferred_element_type=jnp.float32).astype(jnp.bfloat16)
            partial_value = lax.optimization_barrier(partial_value)
            summed = summed + partial_value.astype(jnp.float32)
        live = (jnp.arange(limit, dtype=jnp.int32) < counted).astype(jnp.float32)
        contrib = summed * (weight[picked] * live)[:, None]
        return total.at[picked].add(contrib), None

    start_total = jnp.zeros((TOKENS, D), jnp.float32)
    total, _ = lax.scan(one_expert, start_total, jnp.arange(EXPERTS, dtype=jnp.int32))
    moe_out = total.astype(jnp.bfloat16)

    blocks = REQUESTS // REQ_DEV
    attended = lax.map(attend, (queries.reshape(blocks, REQ_DEV, HEADS, LATENT + ROPE),
                                cache.reshape(blocks, REQ_DEV, MAX_LEN, LATENT + ROPE),
                                lengths.reshape(blocks, REQ_DEV)))
    attention_out = attended.reshape(REQUESTS, HEADS, LATENT)
    return (moe_out, attention_out)
```

```python
import jax
import jax.numpy as jnp
from jax import lax
from jax.sharding import PartitionSpec as P

LATENT = 512
ROPE = 64
NOPE = 128
EXPERTS = 16


def attend(queries, cache, lengths):
    scale = (NOPE + ROPE) ** (-0.5)
    scores = jnp.einsum("rhk,rlk->rhl", queries, cache, preferred_element_type=jnp.float32) * scale
    valid = jnp.arange(cache.shape[1], dtype=jnp.int32)[None, None, :] < lengths[:, None, None]
    scores = jnp.where(valid, scores, -1e30)
    highest = jnp.max(scores, -1, keepdims=True)
    weights = jnp.where(valid, jnp.exp(scores - highest), 0.0)
    probabilities = (weights / jnp.sum(weights, -1, keepdims=True)).astype(jnp.bfloat16)
    return jnp.einsum(
        "rhl,rlk->rhk", probabilities, cache[:, :, :LATENT], preferred_element_type=jnp.float32
    ).astype(jnp.bfloat16)


def per_device(tokens, routes, gates, w_gate, w_up, w_down, queries, cache, lengths):
    axes = ("side", "dev")
    count = lax.axis_size("side") * lax.axis_size("dev")
    slices = count // EXPERTS
    me = lax.axis_index("side") * lax.axis_size("dev") + lax.axis_index("dev")
    expert = me // slices
    dense = jnp.sum(
        jnp.where(
            routes[:, :, None] == jnp.arange(EXPERTS, dtype=jnp.int32)[None, None, :],
            gates[:, :, None],
            0.0,
        ),
        1,
    )
    rows = lax.all_gather(tokens, axes, axis=0, tiled=True)
    weight = lax.all_gather(dense, axes, axis=0, tiled=True)
    own = jnp.sum(jnp.where(jnp.arange(EXPERTS)[None, :] == expert, weight, 0.0), 1)
    gate = jnp.dot(rows, w_gate[0], preferred_element_type=jnp.float32)
    upper = jnp.dot(rows, w_up[0], preferred_element_type=jnp.float32)
    hidden = (jax.nn.silu(gate) * upper).astype(jnp.bfloat16)
    partial = jnp.dot(hidden, w_down[0], preferred_element_type=jnp.float32) * own[:, None]
    moe_out = lax.psum_scatter(
        partial.astype(jnp.bfloat16), axes, scatter_dimension=0, tiled=True
    ).astype(jnp.bfloat16)
    attention_out = attend(queries, cache, lengths)
    return (moe_out, attention_out)


def solution(mesh):
    a = ("side", "dev")
    in_specs = (P(a, None),) * 3 + (P(a, None, None),) * 5 + (P(a),)
    out_specs = (P(a, None), P(a, None, None))
    return jax.shard_map(
        per_device, mesh=mesh, in_specs=in_specs, out_specs=out_specs, check_vma=False
    )
```

```python
import jax
import jax.numpy as jnp
from jax import lax
from jax.experimental import pallas as pl
from jax.experimental.pallas import tpu as pltpu
from jax.sharding import PartitionSpec as P

D = 7168
UNITS = 256
LATENT = 512
KEY = 576
HEADS = 128
MAX_LEN = 1024
REQ = 4
EXPERTS = 16
SCALE = 192.0 ** -0.5

QUARTER = 1792
PIECES = 3
WIDTH = 640
USED = (640, 640, 512)
ROWS = 16
BLOCKS = 64
STAGES = 6
SB_OFF = {5: 0, 4: 512, 3: 768, 2: 896, 1: 960, 0: 992}
MESH = pl.DeviceIdType.MESH
F32 = jnp.float32
BF16 = jnp.bfloat16


def beta_of(p, k, s):
    return s if ((k + p) // 3) % 2 == 0 else 1 - s


def bit_of(c, beta):
    if isinstance(c, int):
        high, low = c // 2, ((c + 1) // 2) % 2
    else:
        high, low = lax.div(c, 2), lax.rem(lax.div(c + 1, 2), 2)
    return beta * high + (1 - beta) * low


def flip_of(c, beta):
    return beta * (3 - c) + (1 - beta) * (c + 1 - 2 * lax.rem(c, 2))


def axis_part(p, s, a, c):
    k = (a - p) % 3
    return bit_of(c, beta_of(p, k, s)) * (1 << k) + bit_of(c, beta_of(p, k + 3, s)) * (1 << (k + 3))


def block_of(p, s, x, y, z):
    return axis_part(p, s, 0, x) + axis_part(p, s, 1, y) + axis_part(p, s, 2, z)


def start_of(n, k):
    return lax.div(n, 1 << k) * (1 << k)


def other_of(n, k):
    return n + (1 << k) * (1 - 2 * lax.rem(lax.div(n, 1 << k), 2))


def rows_of(n, count):
    return pl.ds(pl.multiple_of(n * ROWS, ROWS), count * ROWS)


def gather_plan():
    plan = [(0, -1, 0, False, 0, 1)]
    for k in range(1, STAGES):
        size = 1 << (k - 1)
        parts = 2 if k == 5 else 1
        for new in (False, True):
            for part in range(parts):
                plan.append((k, k - 1 if new else k - 2, k - 1, new, part * (size // parts), size // parts))
    return plan


PLAN = gather_plan()


def plan_region(n, entry):
    k, _, level, new, offset, size = entry
    base = start_of(other_of(n, level), level) if new else start_of(n, level)
    return base + offset, size


def kernel(
    tokens, routes, gates, lengths, w_gate, w_up, w_down, queries, cache,
    moe_out, att_out,
    x_buf, wg, wu, wd, kv, qs, att, acc, hid, gexp, total, sib_out, sib_in, out_buf, in_buf,
    pack, got, pack2, got2,
    local_sem, att_sem, a2a_send, a2a_recv, ag_send, ag_recv, sib_send, sib_recv,
    rsib_send, rsib_recv, rs_send, rs_recv, b2b_send, b2b_recv,
):
    s = lax.axis_index("side")
    dev = lax.axis_index("dev")
    x, y, z = lax.rem(dev, 4), lax.rem(lax.div(dev, 4), 4), lax.div(dev, 16)
    coords = (x, y, z)
    t = 1 - s

    def chip(cx, cy, cz):
        return cz * 16 + cy * 4 + cx

    def partner(p, k):
        a = (k + p) % 3
        new = list(coords)
        new[a] = flip_of(coords[a], beta_of(p, k, s))
        return (s, chip(*new))

    peers = [(s, chip(lax.rem(x + d, 4), y, z)) for d in (1, 2, 3)]
    sibling = (t, dev)

    loads = [
        pltpu.make_async_copy(queries, qs, local_sem.at[0]),
        pltpu.make_async_copy(cache, kv, local_sem.at[1]),
        pltpu.make_async_copy(w_gate.at[0], wg, local_sem.at[2]),
        pltpu.make_async_copy(w_up.at[0], wu, local_sem.at[3]),
        pltpu.make_async_copy(w_down.at[0], wd, local_sem.at[4]),
    ]

    barrier = pltpu.get_barrier_semaphore()
    greet = peers + [sibling] + [
        (s, chip(x, lax.rem(y + 1, 4), z)), (s, chip(x, lax.rem(y + 3, 4), z)),
        (s, chip(x, y, lax.rem(z + 1, 4))), (s, chip(x, y, lax.rem(z + 3, 4))),
    ]
    for who in greet:
        pl.semaphore_signal(barrier, inc=1, device_id=who, device_id_type=MESH)
    for load in loads:
        load.start()

    lane = lax.broadcasted_iota(jnp.int32, (4, 128), 1)
    dense = jnp.zeros((4, 128), F32)
    for k in range(8):
        dense += jnp.where(routes[:, k:k + 1] == (lane & 15), gates[:, k:k + 1], 0.0)
    first = dense.astype(BF16).astype(F32)
    second = (dense - first).astype(BF16).astype(F32)
    third = dense - first - second
    aux = jnp.where(lane < 16, first, jnp.where(lane < 32, second, jnp.where(lane < 48, third, 0.0)))
    aux = jnp.concatenate([aux, jnp.zeros((4, 128), F32)], 1)
    for j in range(4):
        parts = []
        for c in range(4):
            lo = QUARTER * j + 512 * c
            if c < 3:
                parts.append(tokens[:, lo:lo + 512].astype(F32))
            else:
                parts.append(jnp.concatenate([tokens[:, lo:lo + 256].astype(F32), aux], 1))
        pack[j] = jnp.concatenate(parts, 0).astype(BF16)

    pl.semaphore_wait(barrier, len(greet))

    def a2a(src, dst, send, recv):
        copies = []
        for i, who in enumerate(peers):
            to = lax.rem(x + i + 1, 4)
            copies.append(pltpu.make_async_remote_copy(
                src_ref=src.at[to], dst_ref=dst.at[x], send_sem=send.at[i], recv_sem=recv.at[i],
                device_id=who, device_id_type=MESH))
        for copy in copies:
            copy.start()
        dst[x] = src[x]
        return copies

    opened = a2a(pack, got, a2a_send, a2a_recv)
    for copy in opened:
        copy.wait()
    rows = got[...].reshape(64, 512)
    row = lax.broadcasted_iota(jnp.int32, (16, 64), 0)
    col = lax.broadcasted_iota(jnp.int32, (16, 64), 1)
    assembled = []
    for c in range(4):
        select = jnp.where(col == (row >> 2) * 16 + c * 4 + (row & 3), 1.0, 0.0).astype(BF16)
        assembled.append(jnp.dot(select, rows, preferred_element_type=F32).astype(BF16))
    assembled = jnp.concatenate(assembled, 1)

    own = [block_of(p, s, x, y, z) for p in range(PIECES)]
    theirs = [block_of(p, t, x, y, z) for p in range(PIECES)]
    for p in range(PIECES):
        x_buf[s, p, rows_of(own[p], 1), :] = assembled[:, WIDTH * p:WIDTH * (p + 1)]

    def ag_copy(p, i):
        begin, size = plan_region(own[p], PLAN[i])
        region = x_buf.at[s, p, rows_of(begin, size), :]
        return pltpu.make_async_remote_copy(
            src_ref=region, dst_ref=region, send_sem=ag_send.at[p, i], recv_sem=ag_recv.at[p, i],
            device_id=partner(p, PLAN[i][0]), device_id_type=MESH)

    def ag_arrival(p, i):
        begin, size = plan_region(other_of(own[p], PLAN[i][0]), PLAN[i])
        region = x_buf.at[s, p, rows_of(begin, size), :]
        return pltpu.make_async_remote_copy(
            src_ref=region, dst_ref=region, send_sem=ag_send.at[p, i], recv_sem=ag_recv.at[p, i],
            device_id=partner(p, PLAN[i][0]), device_id_type=MESH), begin, size

    final = [i for i in range(len(PLAN)) if PLAN[i][0] == 5]

    def forward_region(p, n, f):
        if f == 0:
            return start_of(n, 3), 8
        if f == 1:
            return start_of(other_of(n, 3), 3), 8
        if f == 2:
            return start_of(other_of(n, 4), 4), 16
        return plan_region(other_of(n, 5), PLAN[final[f - 3]])

    def forward(p, f, n, side):
        begin, size = forward_region(p, n, f)
        region = x_buf.at[side, p, rows_of(begin, size), :]
        return pltpu.make_async_remote_copy(
            src_ref=region, dst_ref=region, send_sem=sib_send.at[p, f], recv_sem=sib_recv.at[p, f],
            device_id=sibling, device_id_type=MESH)

    def ag_start(trigger, p):
        for i, entry in enumerate(PLAN):
            if entry[1] == trigger:
                ag_copy(p, i).start()

    def attend(r):
        scores = lax.dot_general(
            qs[r], kv[r], (((1,), (1,)), ((), ())), preferred_element_type=F32) * SCALE
        valid = lax.broadcasted_iota(jnp.int32, (HEADS, MAX_LEN), 1) < lengths[r]
        scores = jnp.where(valid, scores, -1e30)
        highest = jnp.max(scores, -1, keepdims=True)
        weights = jnp.where(valid, jnp.exp(scores - highest), 0.0)
        chance = (weights / jnp.sum(weights, -1, keepdims=True)).astype(BF16)
        att[r] = jnp.dot(chance, kv[r, :, :LATENT], preferred_element_type=F32).astype(BF16)
        pltpu.make_async_copy(att.at[r], att_out.at[r], att_sem.at[r]).start()

    for p in range(PIECES):
        ag_start(-1, p)
    for k in range(5):
        for p in range(PIECES):
            for i, entry in enumerate(PLAN):
                if entry[0] == k:
                    ag_arrival(p, i)[0].wait_recv()
            ag_start(k, p)
        if k >= 2:
            for p in range(PIECES):
                forward(p, k - 2, own[p], s).start()
        if k == 3:
            loads[0].wait()
            loads[1].wait()
            attend(0)
            attend(1)
        if k == 4:
            attend(2)
            attend(3)
    for f, i in enumerate(final):
        for p in range(PIECES):
            ag_arrival(p, i)[0].wait_recv()
            forward(p, 3 + f, own[p], s).start()

    loads[2].wait()
    loads[3].wait()

    def project(side):
        for p in range(PIECES):
            w = USED[p]

            def step(q, carry):
                base = axis_part(p, side, 0, q)
                tiles = []
                for zz in range(4):
                    for yy in range(4):
                        n = base + axis_part(p, side, 1, yy) + axis_part(p, side, 2, zz)
                        tiles.append(x_buf[side, p, rows_of(n, 1), :w])
                lhs = jnp.concatenate(tiles, 0)
                deep = pl.ds(pl.multiple_of(q * QUARTER + p * WIDTH, 128), w)
                acc[side, :, :UNITS] += jnp.dot(lhs, wg[deep, :], preferred_element_type=F32)
                acc[side, :, UNITS:] += jnp.dot(lhs, wu[deep, :], preferred_element_type=F32)
                return carry

            lax.fori_loop(0, 4, step, 0)
        gate, upper = acc[side, :, :UNITS], acc[side, :, UNITS:]
        hid[side] = (gate / (1.0 + jnp.exp(-gate)) * upper).astype(BF16)
        expert = s * 8 + z * 2 + lax.div(y, 2)
        deep_lane = lax.broadcasted_iota(jnp.int32, (128, 128), 0)
        select = jnp.where(((deep_lane & 15) == expert) & (deep_lane < 48), 1.0, 0.0).astype(BF16)
        tiles = []
        for zz in range(4):
            for yy in range(4):
                n = axis_part(2, side, 1, yy) + axis_part(2, side, 2, zz)
                tiles.append(x_buf[side, 2, rows_of(n, 1), 512:640])
        gexp[side] = jnp.dot(jnp.concatenate(tiles, 0), select, preferred_element_type=F32)

    acc[...] = jnp.zeros_like(acc)
    project(s)
    for p in range(PIECES):
        for f in range(7):
            forward(p, f, theirs[p], t).wait_recv()
    project(t)
    loads[4].wait()

    def down(side, p, put):
        w = USED[p]

        def step(q, carry):
            wide = pl.ds(pl.multiple_of(q * QUARTER + p * WIDTH, 128), w)
            res = jnp.dot(hid[side], wd[:, wide], preferred_element_type=F32)
            res = res * jnp.concatenate([gexp[side]] * (w // 128), 1)
            base = axis_part(p, side, 0, q)
            for zz in range(4):
                for yy in range(4):
                    n = base + axis_part(p, side, 1, yy) + axis_part(p, side, 2, zz)
                    lo = (zz * 4 + yy) * ROWS
                    put(n, res[lo:lo + ROWS])
            return carry

        lax.fori_loop(0, 4, step, 0)

    def half_copy(p, h, n):
        b = lax.rem(lax.div(n, 32), 2)
        begin = (1 - b) * 32 if h == 0 else b * 32
        w = USED[p]
        return pltpu.make_async_remote_copy(
            src_ref=sib_out.at[p, rows_of(begin, 32), pl.ds(0, w)],
            dst_ref=sib_in.at[p, rows_of(begin, 32), pl.ds(0, w)],
            send_sem=rsib_send.at[p, h], recv_sem=rsib_recv.at[p, h],
            device_id=sibling, device_id_type=MESH)

    def rs_copy(p, k):
        region = pl.ds(SB_OFF[k], (1 << k) * ROWS)
        w = USED[p]
        return pltpu.make_async_remote_copy(
            src_ref=out_buf.at[p, region, pl.ds(0, w)], dst_ref=in_buf.at[p, region, pl.ds(0, w)],
            send_sem=rs_send.at[p, k], recv_sem=rs_recv.at[p, k],
            device_id=partner(p, k), device_id_type=MESH)

    for p in range(PIECES):
        def put_out(n, val):
            sib_out[p, rows_of(n, 1), :USED[p]] = val.astype(BF16)
        down(t, p, put_out)
        half_copy(p, 0, theirs[p]).start()
    for p in range(PIECES):
        half_copy(p, 1, theirs[p]).start()
    for p in range(PIECES):
        def put_total(n, val):
            total[p, rows_of(n, 1), :USED[p]] = val
        down(s, p, put_total)

    for p in range(PIECES):
        w = USED[p]
        half_copy(p, 0, own[p]).wait_recv()
        begin = start_of(other_of(own[p], 5), 5)

        def send_half(i, carry):
            at = rows_of(begin + i, 1)
            out_buf[p, pl.ds(pl.multiple_of(i * ROWS, ROWS), ROWS), :w] = (
                total[p, at, :w] + sib_in[p, at, :w].astype(F32)).astype(BF16)
            return carry

        lax.fori_loop(0, 32, send_half, 0)
        rs_copy(p, 5).start()
    for p in range(PIECES):
        w = USED[p]
        half_copy(p, 1, own[p]).wait_recv()
        begin = start_of(own[p], 5)

        def keep_half(i, carry):
            at = rows_of(begin + i, 1)
            total[p, at, :w] += sib_in[p, at, :w].astype(F32)
            return carry

        lax.fori_loop(0, 32, keep_half, 0)
    for k in range(4, -1, -1):
        for p in range(PIECES):
            w = USED[p]
            rs_copy(p, k + 1).wait_recv()
            outer = start_of(own[p], k + 1)
            away, keep = start_of(other_of(own[p], k), k), start_of(own[p], k)

            def send_part(i, carry):
                at = rows_of(away + i, 1)
                came = rows_of(SB_OFF[k + 1] // ROWS + away - outer + i, 1)
                here = pl.ds(pl.multiple_of(SB_OFF[k] + i * ROWS, ROWS), ROWS)
                out_buf[p, here, :w] = (
                    total[p, at, :w] + in_buf[p, came, :w].astype(F32)).astype(BF16)
                return carry

            def keep_part(i, carry):
                at = rows_of(keep + i, 1)
                came = rows_of(SB_OFF[k + 1] // ROWS + keep - outer + i, 1)
                total[p, at, :w] += in_buf[p, came, :w].astype(F32)
                return carry

            lax.fori_loop(0, 1 << k, send_part, 0)
            rs_copy(p, k).start()
            lax.fori_loop(0, 1 << k, keep_part, 0)

    pieces = []
    for p in range(PIECES):
        w = USED[p]
        rs_copy(p, 0).wait_recv()
        pieces.append((total[p, rows_of(own[p], 1), :w]
                       + in_buf[p, pl.ds(SB_OFF[0], ROWS), :w].astype(F32)).astype(BF16))
    pieces.append(jnp.zeros((ROWS, 256), BF16))
    result = jnp.concatenate(pieces, 1)

    row = lax.broadcasted_iota(jnp.int32, (64, 16), 0)
    col = lax.broadcasted_iota(jnp.int32, (64, 16), 1)
    packed = jnp.zeros((64, 512), F32)
    for c in range(4):
        hit = (((row >> 2) & 3) == c) & (col == (row >> 4) * 4 + (row & 3))
        packed += jnp.dot(jnp.where(hit, 1.0, 0.0).astype(BF16), result[:, 512 * c:512 * (c + 1)],
                          preferred_element_type=F32)
    pack2[...] = packed.astype(BF16).reshape(4, 16, 512)
    closed = a2a(pack2, got2, b2b_send, b2b_recv)
    for copy in closed:
        copy.wait()
    row = lax.broadcasted_iota(jnp.int32, (8, 16), 0)
    col = lax.broadcasted_iota(jnp.int32, (8, 16), 1)
    for j in range(4):
        for c in range(4):
            hit = (row < 4) & (col == c * 4 + row)
            value = jnp.dot(jnp.where(hit, 1.0, 0.0).astype(BF16), got2[j], preferred_element_type=F32)
            w = 512 if c < 3 else 256
            lo = QUARTER * j + 512 * c
            moe_out[:, lo:lo + w] = value[:4, :w].astype(BF16)

    for p in range(PIECES):
        for i in range(len(PLAN)):
            ag_copy(p, i).wait_send()
        for f in range(7):
            forward(p, f, own[p], s).wait_send()
        for h in range(2):
            half_copy(p, h, theirs[p]).wait_send()
        for k in range(STAGES):
            rs_copy(p, k).wait_send()
    for r in range(REQ):
        pltpu.make_async_copy(att.at[r], att_out.at[r], att_sem.at[r]).wait()


def per_device(tokens, routes, gates, w_gate, w_up, w_down, queries, cache, lengths):
    vmem = pl.BlockSpec(memory_space=pltpu.VMEM)
    smem = pl.BlockSpec(memory_space=pltpu.SMEM)
    hbm = pl.BlockSpec(memory_space=pl.ANY)
    dma = pltpu.SemaphoreType.DMA
    return pl.pallas_call(
        kernel,
        out_shape=(
            jax.ShapeDtypeStruct((REQ, D), BF16),
            jax.ShapeDtypeStruct((REQ, HEADS, LATENT), BF16),
        ),
        in_specs=[vmem, vmem, vmem, smem, hbm, hbm, hbm, hbm, hbm],
        out_specs=(vmem, hbm),
        scratch_shapes=[
            pltpu.VMEM((2, PIECES, BLOCKS * ROWS, WIDTH), BF16),
            pltpu.VMEM((D, UNITS), BF16),
            pltpu.VMEM((D, UNITS), BF16),
            pltpu.VMEM((UNITS, D), BF16),
            pltpu.VMEM((REQ, MAX_LEN, KEY), BF16),
            pltpu.VMEM((REQ, HEADS, KEY), BF16),
            pltpu.VMEM((REQ, HEADS, LATENT), BF16),
            pltpu.VMEM((2, 256, 2 * UNITS), F32),
            pltpu.VMEM((2, 256, UNITS), BF16),
            pltpu.VMEM((2, 256, 128), F32),
            pltpu.VMEM((PIECES, BLOCKS * ROWS, WIDTH), F32),
            pltpu.VMEM((PIECES, BLOCKS * ROWS, WIDTH), BF16),
            pltpu.VMEM((PIECES, BLOCKS * ROWS, WIDTH), BF16),
            pltpu.VMEM((PIECES, 1008, WIDTH), BF16),
            pltpu.VMEM((PIECES, 1008, WIDTH), BF16),
            pltpu.VMEM((4, 16, 512), BF16),
            pltpu.VMEM((4, 16, 512), BF16),
            pltpu.VMEM((4, 16, 512), BF16),
            pltpu.VMEM((4, 16, 512), BF16),
            dma((5,)), dma((REQ,)), dma((3,)), dma((3,)),
            dma((PIECES, len(PLAN))), dma((PIECES, len(PLAN))),
            dma((PIECES, 7)), dma((PIECES, 7)),
            dma((PIECES, 2)), dma((PIECES, 2)),
            dma((PIECES, STAGES)), dma((PIECES, STAGES)),
            dma((3,)), dma((3,)),
        ],
        compiler_params=pltpu.CompilerParams(
            collective_id=0, has_side_effects=True, vmem_limit_bytes=60 * 1024 * 1024),
    )(tokens, routes, gates, lengths, w_gate, w_up, w_down, queries, cache)


def solution(mesh):
    a = ("side", "dev")
    in_specs = (P(a, None),) * 3 + (P(a, None, None),) * 5 + (P(a),)
    out_specs = (P(a, None), P(a, None, None))
    return jax.shard_map(
        per_device, mesh=mesh, in_specs=in_specs, out_specs=out_specs, check_vma=False
    )
```

```python
import jax
import jax.numpy as jnp
from jax import lax
from jax.experimental import pallas as pl
from jax.experimental.pallas import tpu as pltpu
from jax.sharding import PartitionSpec as P

D = 7168
UNITS = 256
LATENT = 512
KEY = 576
HEADS = 128
MAX_LEN = 1024
REQ = 4
EXPERTS = 16
SCALE = 192.0 ** -0.5

QUARTER = 1792
PIECES = 3
WIDTH = 640
USED = (640, 640, 512)
ROWS = 16
BLOCKS = 64
GROUP = 8
MESH = pl.DeviceIdType.MESH
F32 = jnp.float32
BF16 = jnp.bfloat16


PLAN = ((3, 0, 0), (3, 0, 1), (4, 0, 0), (4, 0, 1), (5, 0, None), (4, 1, None), (5, 1, None),
        (5, 2, None), (5, 3, None))
NEAR = {3: 1, 4: 2, 5: 4}
RETURN = ((5, 4), (5, 5), (5, 6), (5, 7), (4, 2), (4, 3), (3, 1))


def beta_of(p, k, s):
    return s if k < 3 else 1 - s


def bit_of(c, beta):
    if isinstance(c, int):
        high, low = c // 2, ((c + 1) // 2) % 2
    else:
        high, low = lax.div(c, 2), lax.rem(lax.div(c + 1, 2), 2)
    return beta * high + (1 - beta) * low


def flip_of(c, beta):
    return beta * (3 - c) + (1 - beta) * (c + 1 - 2 * lax.rem(c, 2))


def axis_part(p, s, a, c):
    return bit_of(c, s) * (1 << a) + bit_of(c, 1 - s) * (GROUP << ((a - p) % 3))


def block_of(p, s, x, y, z):
    return axis_part(p, s, 0, x) + axis_part(p, s, 1, y) + axis_part(p, s, 2, z)


def flip_bits(n, mask):
    out = n
    for k in range(3):
        if mask >> k & 1:
            out = out + (1 << k) * (1 - 2 * lax.rem(lax.div(n, 1 << k), 2))
    return out


def kernel(
    tokens, routes, gates, lengths, w_gate, w_up, w_down, queries, cache,
    moe_out, att_out,
    x_buf, wg, wu, wd, kv, qs, att, acc, hid, gexp, total, sib_out, sib_in, out_buf, in_buf,
    pack, got, pack2, got2, cube, cube_out, cube_in,
    local_sem, att_sem, a2a_send, a2a_recv, cube_send, cube_recv, ag_send, ag_recv, sib_send, sib_recv,
    rsib_send, rsib_recv, rs_send, rs_recv, back_send, back_recv, b2b_send, b2b_recv,
):
    s = lax.axis_index("side")
    dev = lax.axis_index("dev")
    x, y, z = lax.rem(dev, 4), lax.rem(lax.div(dev, 4), 4), lax.div(dev, 16)
    coords = (x, y, z)
    t = 1 - s

    def chip(cx, cy, cz):
        return cz * 16 + cy * 4 + cx

    def moved(mask, beta):
        return (s, chip(*[flip_of(c, beta) if mask >> a & 1 else c for a, c in enumerate(coords)]))

    def partner(p, k):
        return moved(1 << ((k + p) % 3), 1 - s)

    peers = [(s, chip(lax.rem(x + d, 4), y, z)) for d in (1, 2, 3)]
    sibling = (t, dev)

    loads = [
        pltpu.make_async_copy(queries, qs, local_sem.at[0]),
        pltpu.make_async_copy(cache, kv, local_sem.at[1]),
        pltpu.make_async_copy(w_gate.at[0], wg, local_sem.at[2]),
        pltpu.make_async_copy(w_up.at[0], wu, local_sem.at[3]),
        pltpu.make_async_copy(w_down.at[0], wd, local_sem.at[4]),
    ]

    barrier = pltpu.get_barrier_semaphore()
    greet = [(s, chip(lax.rem(x + 2, 4), y, z)), sibling]
    greet += [moved(mask, s) for mask in range(1, 8)]
    greet += [moved(1 << a, 1 - s) for a in range(3)]
    for who in greet:
        pl.semaphore_signal(barrier, inc=1, device_id=who, device_id_type=MESH)
    for load in loads:
        load.start()

    lane = lax.broadcasted_iota(jnp.int32, (4, 128), 1)
    dense = jnp.zeros((4, 128), F32)
    for k in range(8):
        dense += jnp.where(routes[:, k:k + 1] == (lane & 15), gates[:, k:k + 1], 0.0)
    first = dense.astype(BF16).astype(F32)
    second = (dense - first).astype(BF16).astype(F32)
    third = dense - first - second
    aux = jnp.where(lane < 16, first, jnp.where(lane < 32, second, jnp.where(lane < 48, third, 0.0)))
    aux = jnp.concatenate([aux, jnp.zeros((4, 128), F32)], 1)
    for j in range(4):
        parts = []
        for c in range(4):
            lo = QUARTER * j + 512 * c
            if c < 3:
                parts.append(tokens[:, lo:lo + 512].astype(F32))
            else:
                parts.append(jnp.concatenate([tokens[:, lo:lo + 256].astype(F32), aux], 1))
        pack[j] = jnp.concatenate(parts, 0).astype(BF16)

    pl.semaphore_wait(barrier, len(greet))

    def a2a(src, dst, send, recv):
        copies = []
        for i, who in enumerate(peers):
            to = lax.rem(x + i + 1, 4)
            copies.append(pltpu.make_async_remote_copy(
                src_ref=src.at[to], dst_ref=dst.at[x], send_sem=send.at[i], recv_sem=recv.at[i],
                device_id=who, device_id_type=MESH))
        for copy in copies:
            copy.start()
        dst[x] = src[x]
        return copies

    opened = a2a(pack, got, a2a_send, a2a_recv)
    for copy in opened:
        copy.wait()
    rows = got[...].reshape(64, 512)
    row = lax.broadcasted_iota(jnp.int32, (16, 64), 0)
    col = lax.broadcasted_iota(jnp.int32, (16, 64), 1)
    assembled = []
    for c in range(4):
        select = jnp.where(col == (row >> 2) * 16 + c * 4 + (row & 3), 1.0, 0.0).astype(BF16)
        assembled.append(jnp.dot(select, rows, preferred_element_type=F32).astype(BF16))
    assembled = jnp.concatenate(assembled, 1)

    own = [block_of(p, s, x, y, z) for p in range(PIECES)]
    theirs = [block_of(p, t, x, y, z) for p in range(PIECES)]
    low = lax.rem(own[0], GROUP)
    high = [lax.div(n, GROUP) for n in own]
    high_theirs = [lax.div(n, GROUP) for n in theirs]
    cube[low] = assembled[:, :PIECES * WIDTH]

    def cube_copy(mask):
        return pltpu.make_async_remote_copy(
            src_ref=cube.at[low], dst_ref=cube.at[low],
            send_sem=cube_send.at[mask - 1], recv_sem=cube_recv.at[mask - 1],
            device_id=moved(mask, s), device_id_type=MESH)

    def cube_arrival(mask):
        came = cube.at[flip_bits(low, mask)]
        return pltpu.make_async_remote_copy(
            src_ref=came, dst_ref=came,
            send_sem=cube_send.at[mask - 1], recv_sem=cube_recv.at[mask - 1],
            device_id=moved(mask, s), device_id_type=MESH)

    def half_start(h):
        mine = lax.div(low, 4)
        return 4 * (mine if h == 0 else 1 - mine)

    def ag_copy(p, i):
        k, unit, h = PLAN[i]
        begin, size = (0, 8) if h is None else (half_start(h), 4)
        dst = x_buf.at[s, p, pl.ds(flip_bits(high[p], unit) * GROUP + begin, size)]
        if unit == 0:
            src = cube.at[pl.ds(begin, size), :, pl.ds(p * WIDTH, WIDTH)]
        else:
            src = dst
        return pltpu.make_async_remote_copy(
            src_ref=src, dst_ref=dst, send_sem=ag_send.at[p, i], recv_sem=ag_recv.at[p, i],
            device_id=partner(p, k), device_id_type=MESH)

    def ag_arrival(p, i):
        k, unit, h = PLAN[i]
        begin, size = (0, 8) if h is None else (4 * h, 4)
        came = x_buf.at[s, p, pl.ds(flip_bits(high[p], unit ^ NEAR[k]) * GROUP + begin, size)]
        return pltpu.make_async_remote_copy(
            src_ref=came, dst_ref=came, send_sem=ag_send.at[p, i], recv_sem=ag_recv.at[p, i],
            device_id=partner(p, k), device_id_type=MESH)

    def forward(p, unit, top, side):
        region = x_buf.at[side, p, pl.ds(flip_bits(top, unit) * GROUP, GROUP)]
        return pltpu.make_async_remote_copy(
            src_ref=region, dst_ref=region, send_sem=sib_send.at[p, unit], recv_sem=sib_recv.at[p, unit],
            device_id=sibling, device_id_type=MESH)

    def attend(r):
        scores = jnp.dot(qs[r].T, kv[r], preferred_element_type=F32) * SCALE
        valid = lax.broadcasted_iota(jnp.int32, (HEADS, MAX_LEN), 1) < lengths[r]
        scores = jnp.where(valid, scores, -1e30)
        highest = jnp.max(scores, -1, keepdims=True)
        weights = jnp.where(valid, jnp.exp(scores - highest), 0.0)
        chance = (weights / jnp.sum(weights, -1, keepdims=True)).astype(BF16)
        att[r] = lax.dot_general(
            chance, kv[r, :LATENT, :], (((1,), (1,)), ((), ())), preferred_element_type=F32).astype(BF16)
        pltpu.make_async_copy(att.at[r], att_out.at[r], att_sem.at[r]).start()

    acc[...] = jnp.zeros_like(acc)
    for mask in (7, 3, 5, 6, 1, 2, 4):
        cube_copy(mask).start()
    loads[0].wait()
    loads[1].wait()
    attend(0)
    attend(1)
    for mask in (1, 2, 3):
        cube_arrival(mask).wait_recv()
    for i in (0, 2):
        for p in range(PIECES):
            ag_copy(p, i).start()
    attend(2)
    for mask in (4, 5, 6, 7):
        cube_arrival(mask).wait_recv()
    for i in (1, 3, 4):
        for p in range(PIECES):
            ag_copy(p, i).start()
    for p in range(PIECES):
        x_buf[s, p, pl.ds(high[p] * GROUP, GROUP)] = cube[:, :, WIDTH * p:WIDTH * (p + 1)]
    for p in range(PIECES):
        forward(p, 0, high[p], s).start()
    attend(3)
    for arrived, unit, sent in (((0, 1), 1, (5, 6)), ((2, 3), 2, (7,)), ((5,), 3, (8,))):
        for p in range(PIECES):
            for i in arrived:
                ag_arrival(p, i).wait_recv()
            for i in sent:
                ag_copy(p, i).start()
            forward(p, unit, high[p], s).start()

    def two_of(side, b):
        beta = 1 - side
        return (beta * 2 * b + (1 - beta) * b, beta * (2 * b + 1) + (1 - beta) * (3 - b))

    def project(side, p, b):
        w = USED[p]
        every = (0, 1, 2, 3)
        pair = two_of(side, b)
        zs = pair if p == 0 else every
        ys = pair if p == 2 else every

        def step(i, carry):
            q = pair[0] + i * (pair[1] - pair[0]) if p == 1 else i
            base = axis_part(p, side, 0, q)
            tiles = [
                x_buf[side, p, base + axis_part(p, side, 1, yy) + axis_part(p, side, 2, zz), :, :w]
                for zz in zs for yy in ys]
            lhs = jnp.concatenate(tiles, 0)
            deep = pl.ds(pl.multiple_of(q * QUARTER + p * WIDTH, 128), w)
            for weight, lo in ((wg, 0), (wu, UNITS)):
                res = jnp.dot(lhs, weight[deep, :], preferred_element_type=F32)
                for m, zz in enumerate(zs):
                    for n, yy in enumerate(ys):
                        r = (m * len(ys) + n) * ROWS
                        acc[side, zz * 4 + yy, :, lo:lo + UNITS] += res[r:r + ROWS]
            return carry

        lax.fori_loop(0, 2 if p == 1 else 4, step, 0)

    def bit5(p, side):
        return bit_of(coords[(5 + p) % 3], 1 - side)

    loads[2].wait()
    loads[3].wait()
    for p in range(PIECES):
        project(s, p, bit5(p, s))
    for p in range(PIECES):
        for unit in range(4):
            forward(p, unit, high_theirs[p], t).wait_recv()
        project(t, p, bit5(p, t))
    for unit, i in ((4, 4), (5, 6), (6, 7), (7, 8)):
        for p in range(PIECES):
            ag_arrival(p, i).wait_recv()
            forward(p, unit, high[p], s).start()
    for p in range(PIECES):
        project(s, p, 1 - bit5(p, s))
    for p in range(PIECES):
        for unit in range(4, 8):
            forward(p, unit, high_theirs[p], t).wait_recv()
        project(t, p, 1 - bit5(p, t))

    expert = s * 8 + z * 2 + lax.div(y, 2)
    deep_lane = lax.broadcasted_iota(jnp.int32, (128, 128), 0)
    select = jnp.where(((deep_lane & 15) == expert) & (deep_lane < 48), 1.0, 0.0).astype(BF16)
    for side in (t, s):
        both = acc[side].reshape(256, 2 * UNITS)
        gate, upper = both[:, :UNITS], both[:, UNITS:]
        hid[side] = (gate / (1.0 + jnp.exp(-gate)) * upper).astype(BF16)
        tiles = [
            x_buf[side, 2, axis_part(2, side, 1, yy) + axis_part(2, side, 2, zz), :, 512:640]
            for zz in range(4) for yy in range(4)]
        gexp[side] = jnp.dot(jnp.concatenate(tiles, 0), select, preferred_element_type=F32)
    loads[4].wait()

    def down(side, p, put):
        w = USED[p]

        def step(q, carry):
            wide = pl.ds(pl.multiple_of(q * QUARTER + p * WIDTH, 128), w)
            res = jnp.dot(hid[side], wd[:, wide], preferred_element_type=F32)
            res = res * jnp.concatenate([gexp[side]] * (w // 128), 1)
            base = axis_part(p, side, 0, q)
            for zz in range(4):
                for yy in range(4):
                    n = base + axis_part(p, side, 1, yy) + axis_part(p, side, 2, zz)
                    lo = (zz * 4 + yy) * ROWS
                    put(n, res[lo:lo + ROWS])
            return carry

        lax.fori_loop(0, 4, step, 0)

    def half_copy(p, h, n):
        b = lax.div(n, 32)
        begin = (1 - b) * 32 if h == 0 else b * 32
        w = USED[p]
        return pltpu.make_async_remote_copy(
            src_ref=sib_out.at[p, pl.ds(begin, 32), :, pl.ds(0, w)],
            dst_ref=sib_in.at[p, pl.ds(begin, 32), :, pl.ds(0, w)],
            send_sem=rsib_send.at[p, h], recv_sem=rsib_recv.at[p, h],
            device_id=sibling, device_id_type=MESH)

    def rs_copy(p, i):
        w = USED[p]
        return pltpu.make_async_remote_copy(
            src_ref=out_buf.at[p, i, :, :, pl.ds(0, w)], dst_ref=in_buf.at[p, i, :, :, pl.ds(0, w)],
            send_sem=rs_send.at[p, i], recv_sem=rs_recv.at[p, i],
            device_id=partner(p, RETURN[i][0]), device_id_type=MESH)

    def came_for(unit):
        return [] if unit > 3 else [unit] + ([4 + unit] if unit < 2 else []) + ([6] if unit < 1 else [])

    def summed(p, unit, j):
        w = USED[p]
        n = flip_bits(high[p], unit) * GROUP + j
        value = total[p, n, :, :w] + sib_in[p, n, :, :w].astype(F32)
        for slot in came_for(unit):
            value += in_buf[p, slot, j, :, :w].astype(F32)
        return value

    def give(p, i):
        def step(j, carry):
            out_buf[p, i, j, :, :USED[p]] = summed(p, RETURN[i][1], j).astype(BF16)
            return carry

        lax.fori_loop(0, GROUP, step, 0)
        rs_copy(p, i).start()

    for p in range(PIECES):
        def put_out(n, val):
            sib_out[p, n, :, :USED[p]] = val.astype(BF16)
        down(t, p, put_out)
        half_copy(p, 0, theirs[p]).start()
    for p in range(PIECES):
        half_copy(p, 1, theirs[p]).start()
    for p in range(PIECES):
        def put_total(n, val):
            total[p, n, :, :USED[p]] = val
        down(s, p, put_total)
        half_copy(p, 0, own[p]).wait_recv()
        for i in (3, 2, 1, 0):
            give(p, i)
    for p in range(PIECES):
        half_copy(p, 1, own[p]).wait_recv()
    for i, before in ((5, (3,)), (4, (2,)), (6, (1, 5))):
        for p in range(PIECES):
            for slot in before:
                rs_copy(p, slot).wait_recv()
            give(p, i)
    for p in range(PIECES):
        for slot in (0, 4, 6):
            rs_copy(p, slot).wait_recv()

    def back_copy(mask):
        return pltpu.make_async_remote_copy(
            src_ref=cube_out.at[flip_bits(low, mask)], dst_ref=cube_in.at[low],
            send_sem=back_send.at[mask - 1], recv_sem=back_recv.at[mask - 1],
            device_id=moved(mask, s), device_id_type=MESH)

    def back_arrival(mask):
        came = cube_in.at[flip_bits(low, mask)]
        return pltpu.make_async_remote_copy(
            src_ref=came, dst_ref=came,
            send_sem=back_send.at[mask - 1], recv_sem=back_recv.at[mask - 1],
            device_id=moved(mask, s), device_id_type=MESH)

    for mask in (7, 3, 5, 6, 1, 2, 4):
        to = flip_bits(low, mask)
        for p in range(PIECES):
            cube_out[to, :, WIDTH * p:WIDTH * p + USED[p]] = summed(p, 0, to).astype(BF16)
        back_copy(mask).start()
    result = jnp.concatenate([summed(p, 0, low) for p in range(PIECES)], 1)
    for mask in (4, 2, 1, 6, 5, 3, 7):
        back_arrival(mask).wait_recv()
        result += cube_in[flip_bits(low, mask)].astype(F32)
    result = jnp.concatenate([result.astype(BF16), jnp.zeros((ROWS, 256), BF16)], 1)

    row = lax.broadcasted_iota(jnp.int32, (64, 16), 0)
    col = lax.broadcasted_iota(jnp.int32, (64, 16), 1)
    packed = jnp.zeros((64, 512), F32)
    for c in range(4):
        hit = (((row >> 2) & 3) == c) & (col == (row >> 4) * 4 + (row & 3))
        packed += jnp.dot(jnp.where(hit, 1.0, 0.0).astype(BF16), result[:, 512 * c:512 * (c + 1)],
                          preferred_element_type=F32)
    pack2[...] = packed.astype(BF16).reshape(4, 16, 512)
    closed = a2a(pack2, got2, b2b_send, b2b_recv)
    for copy in closed:
        copy.wait()
    row = lax.broadcasted_iota(jnp.int32, (8, 16), 0)
    col = lax.broadcasted_iota(jnp.int32, (8, 16), 1)
    for j in range(4):
        for c in range(4):
            hit = (row < 4) & (col == c * 4 + row)
            value = jnp.dot(jnp.where(hit, 1.0, 0.0).astype(BF16), got2[j], preferred_element_type=F32)
            w = 512 if c < 3 else 256
            lo = QUARTER * j + 512 * c
            moe_out[:, lo:lo + w] = value[:4, :w].astype(BF16)

    for mask in range(1, 8):
        cube_copy(mask).wait_send()
        back_copy(mask).wait_send()
    for p in range(PIECES):
        for i in range(len(PLAN)):
            ag_copy(p, i).wait_send()
        for unit in range(8):
            forward(p, unit, high[p], s).wait_send()
        for h in range(2):
            half_copy(p, h, theirs[p]).wait_send()
        for i in range(len(RETURN)):
            rs_copy(p, i).wait_send()
    for r in range(REQ):
        pltpu.make_async_copy(att.at[r], att_out.at[r], att_sem.at[r]).wait()


def per_device(tokens, routes, gates, w_gate, w_up, w_down, queries, cache, lengths):
    vmem = pl.BlockSpec(memory_space=pltpu.VMEM)
    smem = pl.BlockSpec(memory_space=pltpu.SMEM)
    hbm = pl.BlockSpec(memory_space=pl.ANY)
    dma = pltpu.SemaphoreType.DMA
    return pl.pallas_call(
        kernel,
        out_shape=(
            jax.ShapeDtypeStruct((REQ, D), BF16),
            jax.ShapeDtypeStruct((REQ, HEADS, LATENT), BF16),
        ),
        in_specs=[vmem, vmem, vmem, smem, hbm, hbm, hbm, hbm, hbm],
        out_specs=(vmem, hbm),
        scratch_shapes=[
            pltpu.VMEM((2, PIECES, BLOCKS, ROWS, WIDTH), BF16),
            pltpu.VMEM((D, UNITS), BF16),
            pltpu.VMEM((D, UNITS), BF16),
            pltpu.VMEM((UNITS, D), BF16),
            pltpu.VMEM((REQ, KEY, MAX_LEN), BF16),
            pltpu.VMEM((REQ, KEY, HEADS), BF16),
            pltpu.VMEM((REQ, HEADS, LATENT), BF16),
            pltpu.VMEM((2, 16, ROWS, 2 * UNITS), F32),
            pltpu.VMEM((2, 256, UNITS), BF16),
            pltpu.VMEM((2, 256, 128), F32),
            pltpu.VMEM((PIECES, BLOCKS, ROWS, WIDTH), F32),
            pltpu.VMEM((PIECES, BLOCKS, ROWS, WIDTH), BF16),
            pltpu.VMEM((PIECES, BLOCKS, ROWS, WIDTH), BF16),
            pltpu.VMEM((PIECES, len(RETURN), GROUP, ROWS, WIDTH), BF16),
            pltpu.VMEM((PIECES, len(RETURN), GROUP, ROWS, WIDTH), BF16),
            pltpu.VMEM((4, 16, 512), BF16),
            pltpu.VMEM((4, 16, 512), BF16),
            pltpu.VMEM((4, 16, 512), BF16),
            pltpu.VMEM((4, 16, 512), BF16),
            pltpu.VMEM((GROUP, ROWS, PIECES * WIDTH), BF16),
            pltpu.VMEM((GROUP, ROWS, QUARTER), BF16),
            pltpu.VMEM((GROUP, ROWS, QUARTER), BF16),
            dma((5,)), dma((REQ,)), dma((3,)), dma((3,)), dma((7,)), dma((7,)),
            dma((PIECES, len(PLAN))), dma((PIECES, len(PLAN))),
            dma((PIECES, 8)), dma((PIECES, 8)),
            dma((PIECES, 2)), dma((PIECES, 2)),
            dma((PIECES, len(RETURN))), dma((PIECES, len(RETURN))), dma((7,)), dma((7,)),
            dma((3,)), dma((3,)),
        ],
        compiler_params=pltpu.CompilerParams(
            collective_id=0, has_side_effects=True, vmem_limit_bytes=60 * 1024 * 1024),
    )(tokens, routes, gates, lengths, w_gate, w_up, w_down,
      queries.transpose(0, 2, 1), cache.transpose(0, 2, 1))


def solution(mesh):
    a = ("side", "dev")
    in_specs = (P(a, None),) * 3 + (P(a, None, None),) * 5 + (P(a),)
    out_specs = (P(a, None), P(a, None, None))
    return jax.shard_map(
        per_device, mesh=mesh, in_specs=in_specs, out_specs=out_specs, check_vma=False
    )
```

```python
import jax
import jax.numpy as jnp
from jax import lax
from jax.experimental import pallas as pl
from jax.experimental.pallas import tpu as pltpu
from jax.sharding import PartitionSpec as P

D = 7168
UNITS = 256
LATENT = 512
KEY = 576
HEADS = 128
MAX_LEN = 1024
REQ = 4
EXPERTS = 16
SCALE = 192.0 ** -0.5

QUARTER = 1792
PIECES = 3
UNROLL = True
WIDTH = 640
USED = (640, 640, 512)
ROWS = 16
BLOCKS = 64
GROUP = 8
MESH = pl.DeviceIdType.MESH
F32 = jnp.float32
BF16 = jnp.bfloat16


PLAN = ((3, 0, 0), (3, 0, 1), (4, 0, 0), (4, 0, 1), (5, 0, 0), (4, 1, None), (5, 1, None),
        (5, 2, None), (5, 3, None), (5, 0, 1))
NEAR = {3: 1, 4: 2, 5: 4}
RETURN = ((5, 4), (5, 5), (5, 6), (5, 7), (4, 2), (4, 3), (3, 1))


def beta_of(p, k, s):
    return s if k < 3 else 1 - s


def bit_of(c, beta):
    if isinstance(c, int):
        high, low = c // 2, ((c + 1) // 2) % 2
    else:
        high, low = lax.div(c, 2), lax.rem(lax.div(c + 1, 2), 2)
    return beta * high + (1 - beta) * low


def flip_of(c, beta):
    return beta * (3 - c) + (1 - beta) * (c + 1 - 2 * lax.rem(c, 2))


def axis_part(p, s, a, c):
    return bit_of(c, s) * (1 << a) + bit_of(c, 1 - s) * (GROUP << ((a - p) % 3))


def block_of(p, s, x, y, z):
    return axis_part(p, s, 0, x) + axis_part(p, s, 1, y) + axis_part(p, s, 2, z)


def flip_bits(n, mask):
    out = n
    for k in range(3):
        if mask >> k & 1:
            out = out + (1 << k) * (1 - 2 * lax.rem(lax.div(n, 1 << k), 2))
    return out


def kernel(
    tokens, routes, gates, lengths, w_gate, w_up, w_down, queries, cache,
    got2, att_out,
    x_buf, wg, wu, wd, kv, qs, att, acc, hid, gexp, total, sib_out, sib_in, out_buf, in_buf,
    pack, got, pack2, cube, cube_out, cube_in,
    local_sem, att_sem, a2a_send, a2a_recv, cube_send, cube_recv, ag_send, ag_recv, sib_send, sib_recv,
    rsib_send, rsib_recv, rs_send, rs_recv, back_send, back_recv, b2b_send, b2b_recv,
):
    s = lax.axis_index("side")
    dev = lax.axis_index("dev")
    x, y, z = lax.rem(dev, 4), lax.rem(lax.div(dev, 4), 4), lax.div(dev, 16)
    coords = (x, y, z)
    t = 1 - s

    def chip(cx, cy, cz):
        return cz * 16 + cy * 4 + cx

    def moved(mask, beta):
        return (s, chip(*[flip_of(c, beta) if mask >> a & 1 else c for a, c in enumerate(coords)]))

    def partner(p, k):
        return moved(1 << ((k + p) % 3), 1 - s)

    peers = [(s, chip(lax.rem(x + d, 4), y, z)) for d in (1, 2, 3)]
    sibling = (t, dev)

    loads = [
        pltpu.make_async_copy(queries, qs, local_sem.at[0]),
        pltpu.make_async_copy(cache, kv, local_sem.at[1]),
        pltpu.make_async_copy(w_gate.at[0], wg, local_sem.at[2]),
        pltpu.make_async_copy(w_up.at[0], wu, local_sem.at[3]),
        pltpu.make_async_copy(w_down.at[0], wd, local_sem.at[4]),
    ]

    barrier = pltpu.get_barrier_semaphore()
    greet = [(s, chip(lax.rem(x + 2, 4), y, z)), sibling]
    greet += [moved(mask, s) for mask in range(1, 8)]
    greet += [moved(1 << a, 1 - s) for a in range(3)]
    for who in greet:
        pl.semaphore_signal(barrier, inc=1, device_id=who, device_id_type=MESH)
    for load in loads:
        load.start()

    lane = lax.broadcasted_iota(jnp.int32, (4, 128), 1)
    dense = jnp.zeros((4, 128), F32)
    for k in range(8):
        dense += jnp.where(routes[:, k:k + 1] == (lane & 15), gates[:, k:k + 1], 0.0)
    first = dense.astype(BF16).astype(F32)
    second = (dense - first).astype(BF16).astype(F32)
    third = dense - first - second
    aux = jnp.where(lane < 16, first, jnp.where(lane < 32, second, jnp.where(lane < 48, third, 0.0)))
    aux = jnp.concatenate([aux, jnp.zeros((4, 128), F32)], 1)
    for j in range(4):
        parts = []
        for c in range(4):
            lo = QUARTER * j + 512 * c
            if c < 3:
                parts.append(tokens[:, lo:lo + 512].astype(F32))
            else:
                parts.append(jnp.concatenate([tokens[:, lo:lo + 256].astype(F32), aux], 1))
        pack[j] = jnp.concatenate(parts, 0).astype(BF16)

    pl.semaphore_wait(barrier, len(greet))

    def a2a(src, dst, send, recv):
        copies = []
        for i, who in enumerate(peers):
            to = lax.rem(x + i + 1, 4)
            copies.append(pltpu.make_async_remote_copy(
                src_ref=src.at[to], dst_ref=dst.at[x], send_sem=send.at[i], recv_sem=recv.at[i],
                device_id=who, device_id_type=MESH))
        for copy in copies:
            copy.start()
        dst[x] = src[x]
        return copies

    opened = a2a(pack, got, a2a_send, a2a_recv)
    for copy in opened:
        copy.wait()
    rows = got[...].reshape(64, 512)
    row = lax.broadcasted_iota(jnp.int32, (16, 64), 0)
    col = lax.broadcasted_iota(jnp.int32, (16, 64), 1)
    assembled = []
    for c in range(4):
        select = jnp.where(col == (row >> 2) * 16 + c * 4 + (row & 3), 1.0, 0.0).astype(BF16)
        assembled.append(jnp.dot(select, rows, preferred_element_type=F32).astype(BF16))
    assembled = jnp.concatenate(assembled, 1)

    own = [block_of(p, s, x, y, z) for p in range(PIECES)]
    theirs = [block_of(p, t, x, y, z) for p in range(PIECES)]
    low = lax.rem(own[0], GROUP)
    high = [lax.div(n, GROUP) for n in own]
    high_theirs = [lax.div(n, GROUP) for n in theirs]
    cube[low] = assembled[:, :PIECES * WIDTH]

    def cube_copy(mask):
        return pltpu.make_async_remote_copy(
            src_ref=cube.at[low], dst_ref=cube.at[low],
            send_sem=cube_send.at[mask - 1], recv_sem=cube_recv.at[mask - 1],
            device_id=moved(mask, s), device_id_type=MESH)

    def cube_arrival(mask):
        came = cube.at[flip_bits(low, mask)]
        return pltpu.make_async_remote_copy(
            src_ref=came, dst_ref=came,
            send_sem=cube_send.at[mask - 1], recv_sem=cube_recv.at[mask - 1],
            device_id=moved(mask, s), device_id_type=MESH)

    def half_start(h):
        mine = lax.div(low, 4)
        return 4 * (mine if h == 0 else 1 - mine)

    def ag_copy(p, i):
        k, unit, h = PLAN[i]
        begin, size = (0, 8) if h is None else (half_start(h), 4)
        dst = x_buf.at[s, p, pl.ds(flip_bits(high[p], unit) * GROUP + begin, size)]
        if unit == 0:
            src = cube.at[pl.ds(begin, size), :, pl.ds(p * WIDTH, WIDTH)]
        else:
            src = dst
        return pltpu.make_async_remote_copy(
            src_ref=src, dst_ref=dst, send_sem=ag_send.at[p, i], recv_sem=ag_recv.at[p, i],
            device_id=partner(p, k), device_id_type=MESH)

    def ag_arrival(p, i):
        k, unit, h = PLAN[i]
        begin, size = (0, 8) if h is None else (4 * h, 4)
        came = x_buf.at[s, p, pl.ds(flip_bits(high[p], unit ^ NEAR[k]) * GROUP + begin, size)]
        return pltpu.make_async_remote_copy(
            src_ref=came, dst_ref=came, send_sem=ag_send.at[p, i], recv_sem=ag_recv.at[p, i],
            device_id=partner(p, k), device_id_type=MESH)

    def forward(p, unit, top, side):
        region = x_buf.at[side, p, pl.ds(flip_bits(top, unit) * GROUP, GROUP)]
        return pltpu.make_async_remote_copy(
            src_ref=region, dst_ref=region, send_sem=sib_send.at[p, unit], recv_sem=sib_recv.at[p, unit],
            device_id=sibling, device_id_type=MESH)

    def attend(r):
        scores = jnp.dot(qs[r].T, kv[r], preferred_element_type=F32) * SCALE
        valid = lax.broadcasted_iota(jnp.int32, (HEADS, MAX_LEN), 1) < lengths[r]
        scores = jnp.where(valid, scores, -1e30)
        highest = jnp.max(scores, -1, keepdims=True)
        weights = jnp.where(valid, jnp.exp(scores - highest), 0.0)
        chance = (weights / jnp.sum(weights, -1, keepdims=True)).astype(BF16)
        att[r] = lax.dot_general(
            chance, kv[r, :LATENT, :], (((1,), (1,)), ((), ())), preferred_element_type=F32).astype(BF16)
        pltpu.make_async_copy(att.at[r], att_out.at[r], att_sem.at[r]).start()

    acc[...] = jnp.zeros_like(acc)
    for mask in (3, 1, 2, 7, 5, 6, 4):
        cube_copy(mask).start()
    loads[0].wait()
    loads[1].wait()
    attend(0)
    attend(1)
    for mask in (1, 2, 3):
        cube_arrival(mask).wait_recv()
    for i in (0, 2, 4):
        for p in range(PIECES):
            ag_copy(p, i).start()
    attend(2)
    for mask in (4, 5, 6, 7):
        cube_arrival(mask).wait_recv()
    for i in (1, 3, 9):
        for p in range(PIECES):
            ag_copy(p, i).start()
    for p in range(PIECES):
        x_buf[s, p, pl.ds(high[p] * GROUP, GROUP)] = cube[:, :, WIDTH * p:WIDTH * (p + 1)]
    for p in range(PIECES):
        forward(p, 0, high[p], s).start()
    attend(3)
    for arrived, unit, sent in (((0, 1), 1, (5, 6)), ((2, 3), 2, (7,)), ((5,), 3, (8,))):
        for p in range(PIECES):
            for i in arrived:
                ag_arrival(p, i).wait_recv()
            for i in sent:
                ag_copy(p, i).start()
            forward(p, unit, high[p], s).start()

    def two_of(side, b):
        beta = 1 - side
        return (beta * 2 * b + (1 - beta) * b, beta * (2 * b + 1) + (1 - beta) * (3 - b))

    def project(side, p, b):
        w = USED[p]
        every = (0, 1, 2, 3)
        pair = two_of(side, b)
        zs = pair if p == 0 else every
        ys = pair if p == 2 else every

        def step(i, carry):
            q = pair[0] + i * (pair[1] - pair[0]) if p == 1 else i
            base = axis_part(p, side, 0, q)
            tiles = [
                x_buf[side, p, base + axis_part(p, side, 1, yy) + axis_part(p, side, 2, zz), :, :w]
                for zz in zs for yy in ys]
            lhs = jnp.concatenate(tiles, 0)
            deep = pl.ds(pl.multiple_of(q * QUARTER + p * WIDTH, 128), w)
            for weight, lo in ((wg, 0), (wu, UNITS)):
                res = jnp.dot(lhs, weight[deep, :], preferred_element_type=F32)
                for m, zz in enumerate(zs):
                    for n, yy in enumerate(ys):
                        r = (m * len(ys) + n) * ROWS
                        acc[side, zz * 4 + yy, :, lo:lo + UNITS] += res[r:r + ROWS]
            return carry

        lax.fori_loop(0, 2 if p == 1 else 4, step, 0, unroll=UNROLL)

    def bit5(p, side):
        return bit_of(coords[(5 + p) % 3], 1 - side)

    loads[2].wait()
    loads[3].wait()
    for p in range(PIECES):
        project(s, p, bit5(p, s))
    for p in range(PIECES):
        for unit in range(4):
            forward(p, unit, high_theirs[p], t).wait_recv()
        project(t, p, bit5(p, t))
    for unit, arrived in ((4, (4, 9)), (5, (6,)), (6, (7,)), (7, (8,))):
        for p in range(PIECES):
            for i in arrived:
                ag_arrival(p, i).wait_recv()
            forward(p, unit, high[p], s).start()
    for p in range(PIECES):
        project(s, p, 1 - bit5(p, s))
    for p in range(PIECES):
        for unit in range(4, 8):
            forward(p, unit, high_theirs[p], t).wait_recv()
        project(t, p, 1 - bit5(p, t))

    expert = s * 8 + z * 2 + lax.div(y, 2)
    deep_lane = lax.broadcasted_iota(jnp.int32, (128, 128), 0)
    select = jnp.where(((deep_lane & 15) == expert) & (deep_lane < 48), 1.0, 0.0).astype(BF16)
    for side in (t, s):
        both = acc[side].reshape(256, 2 * UNITS)
        gate, upper = both[:, :UNITS], both[:, UNITS:]
        hid[side] = (gate / (1.0 + jnp.exp(-gate)) * upper).astype(BF16).reshape(16, ROWS, UNITS)
        tiles = [
            x_buf[side, 2, axis_part(2, side, 1, yy) + axis_part(2, side, 2, zz), :, 512:640]
            for zz in range(4) for yy in range(4)]
        gexp[side] = jnp.dot(
            jnp.concatenate(tiles, 0), select, preferred_element_type=F32).reshape(16, ROWS, 128)
    loads[4].wait()

    def down(side, p, b, put):
        w = USED[p]
        every = (0, 1, 2, 3)
        pair = two_of(side, b)
        zs = pair if p == 0 else every
        ys = pair if p == 2 else every
        lhs = jnp.concatenate([hid[side, zz * 4 + yy] for zz in zs for yy in ys], 0)
        share = jnp.concatenate([gexp[side, zz * 4 + yy] for zz in zs for yy in ys], 0)
        share = jnp.concatenate([share] * (w // 128), 1)

        def step(i, carry):
            q = pair[0] + i * (pair[1] - pair[0]) if p == 1 else i
            wide = pl.ds(pl.multiple_of(q * QUARTER + p * WIDTH, 128), w)
            res = jnp.dot(lhs, wd[:, wide], preferred_element_type=F32) * share
            base = axis_part(p, side, 0, q)
            for m, zz in enumerate(zs):
                for n, yy in enumerate(ys):
                    r = (m * len(ys) + n) * ROWS
                    put(base + axis_part(p, side, 1, yy) + axis_part(p, side, 2, zz), res[r:r + ROWS])
            return carry

        lax.fori_loop(0, 2 if p == 1 else 4, step, 0, unroll=UNROLL)

    def half_copy(p, h, n):
        b = lax.div(n, 32)
        begin = (1 - b) * 32 if h == 0 else b * 32
        w = USED[p]
        return pltpu.make_async_remote_copy(
            src_ref=sib_out.at[p, pl.ds(begin, 32), :, pl.ds(0, w)],
            dst_ref=sib_in.at[p, pl.ds(begin, 32), :, pl.ds(0, w)],
            send_sem=rsib_send.at[p, h], recv_sem=rsib_recv.at[p, h],
            device_id=sibling, device_id_type=MESH)

    def rs_copy(p, i):
        w = USED[p]
        return pltpu.make_async_remote_copy(
            src_ref=out_buf.at[p, i, :, :, pl.ds(0, w)], dst_ref=in_buf.at[p, i, :, :, pl.ds(0, w)],
            send_sem=rs_send.at[p, i], recv_sem=rs_recv.at[p, i],
            device_id=partner(p, RETURN[i][0]), device_id_type=MESH)

    def came_for(unit):
        return [] if unit > 3 else [unit] + ([4 + unit] if unit < 2 else []) + ([6] if unit < 1 else [])

    def summed(p, unit, j):
        w = USED[p]
        n = flip_bits(high[p], unit) * GROUP + j
        value = total[p, n, :, :w] + sib_in[p, n, :, :w].astype(F32)
        for slot in came_for(unit):
            value += in_buf[p, slot, j, :, :w].astype(F32)
        return value

    def give(p, i):
        def step(j, carry):
            out_buf[p, i, j, :, :USED[p]] = summed(p, RETURN[i][1], j).astype(BF16)
            return carry

        lax.fori_loop(0, GROUP, step, 0)
        rs_copy(p, i).start()

    def put_out(p):
        def put(n, val):
            sib_out[p, n, :, :USED[p]] = val.astype(BF16)
        return put

    def put_total(p):
        def put(n, val):
            total[p, n, :, :USED[p]] = val
        return put

    for p in range(PIECES):
        down(t, p, 1 - bit5(p, t), put_out(p))
        half_copy(p, 0, theirs[p]).start()
    for p in range(PIECES):
        down(s, p, 1 - bit5(p, s), put_total(p))
        half_copy(p, 0, own[p]).wait_recv()
        for i in (3, 2, 1, 0):
            give(p, i)
    for p in range(PIECES):
        down(t, p, bit5(p, t), put_out(p))
        half_copy(p, 1, theirs[p]).start()
    for p in range(PIECES):
        down(s, p, bit5(p, s), put_total(p))
        half_copy(p, 1, own[p]).wait_recv()
    for i, before in ((5, (3,)), (4, (2,)), (6, (1, 5))):
        for p in range(PIECES):
            for slot in before:
                rs_copy(p, slot).wait_recv()
            give(p, i)
    for p in range(PIECES):
        for slot in (0, 4, 6):
            rs_copy(p, slot).wait_recv()

    def back_copy(mask):
        return pltpu.make_async_remote_copy(
            src_ref=cube_out.at[flip_bits(low, mask)], dst_ref=cube_in.at[low],
            send_sem=back_send.at[mask - 1], recv_sem=back_recv.at[mask - 1],
            device_id=moved(mask, s), device_id_type=MESH)

    def back_arrival(mask):
        came = cube_in.at[flip_bits(low, mask)]
        return pltpu.make_async_remote_copy(
            src_ref=came, dst_ref=came,
            send_sem=back_send.at[mask - 1], recv_sem=back_recv.at[mask - 1],
            device_id=moved(mask, s), device_id_type=MESH)

    for mask in (7, 3, 5, 6, 1, 2, 4):
        to = flip_bits(low, mask)
        for p in range(PIECES):
            cube_out[to, :, WIDTH * p:WIDTH * p + USED[p]] = summed(p, 0, to).astype(BF16)
        back_copy(mask).start()
    result = jnp.concatenate([summed(p, 0, low) for p in range(PIECES)], 1)
    for mask in (4, 2, 1, 6, 5, 3, 7):
        back_arrival(mask).wait_recv()
        result += cube_in[flip_bits(low, mask)].astype(F32)
    result = jnp.concatenate([result.astype(BF16), jnp.zeros((ROWS, 256), BF16)], 1)

    row = lax.broadcasted_iota(jnp.int32, (64, 16), 0)
    col = lax.broadcasted_iota(jnp.int32, (64, 16), 1)
    packed = jnp.zeros((64, 512), F32)
    for c in range(4):
        hit = (((row >> 2) & 3) == c) & (col == (row >> 4) * 4 + (row & 3))
        packed += jnp.dot(jnp.where(hit, 1.0, 0.0).astype(BF16), result[:, 512 * c:512 * (c + 1)],
                          preferred_element_type=F32)
    pack2[...] = packed.astype(BF16).reshape(4, 16, 512)
    closed = a2a(pack2, got2, b2b_send, b2b_recv)
    for copy in closed:
        copy.wait()
    for mask in range(1, 8):
        cube_copy(mask).wait_send()
        back_copy(mask).wait_send()
    for p in range(PIECES):
        for i in range(len(PLAN)):
            ag_copy(p, i).wait_send()
        for unit in range(8):
            forward(p, unit, high[p], s).wait_send()
        for h in range(2):
            half_copy(p, h, theirs[p]).wait_send()
        for i in range(len(RETURN)):
            rs_copy(p, i).wait_send()
    for r in range(REQ):
        pltpu.make_async_copy(att.at[r], att_out.at[r], att_sem.at[r]).wait()


def finish(got, att, moe_out, att_out):
    att_out[...] = att[...]
    row = lax.broadcasted_iota(jnp.int32, (8, 16), 0)
    col = lax.broadcasted_iota(jnp.int32, (8, 16), 1)
    for j in range(4):
        for c in range(4):
            hit = (row < 4) & (col == c * 4 + row)
            value = jnp.dot(jnp.where(hit, 1.0, 0.0).astype(BF16), got[j], preferred_element_type=F32)
            w = 512 if c < 3 else 256
            lo = QUARTER * j + 512 * c
            moe_out[:, lo:lo + w] = value[:4, :w].astype(BF16)


def per_device(tokens, routes, gates, w_gate, w_up, w_down, queries, cache, lengths):
    vmem = pl.BlockSpec(memory_space=pltpu.VMEM)
    smem = pl.BlockSpec(memory_space=pltpu.SMEM)
    hbm = pl.BlockSpec(memory_space=pl.ANY)
    dma = pltpu.SemaphoreType.DMA
    got, att = pl.pallas_call(
        kernel,
        out_shape=(
            jax.ShapeDtypeStruct((4, 16, 512), BF16),
            jax.ShapeDtypeStruct((REQ, HEADS, LATENT), BF16),
        ),
        in_specs=[vmem, vmem, vmem, smem, hbm, hbm, hbm, hbm, hbm],
        out_specs=(vmem, hbm),
        scratch_shapes=[
            pltpu.VMEM((2, PIECES, BLOCKS, ROWS, WIDTH), BF16),
            pltpu.VMEM((D, UNITS), BF16),
            pltpu.VMEM((D, UNITS), BF16),
            pltpu.VMEM((UNITS, D), BF16),
            pltpu.VMEM((REQ, KEY, MAX_LEN), BF16),
            pltpu.VMEM((REQ, KEY, HEADS), BF16),
            pltpu.VMEM((REQ, HEADS, LATENT), BF16),
            pltpu.VMEM((2, 16, ROWS, 2 * UNITS), F32),
            pltpu.VMEM((2, 16, ROWS, UNITS), BF16),
            pltpu.VMEM((2, 16, ROWS, 128), F32),
            pltpu.VMEM((PIECES, BLOCKS, ROWS, WIDTH), F32),
            pltpu.VMEM((PIECES, BLOCKS, ROWS, WIDTH), BF16),
            pltpu.VMEM((PIECES, BLOCKS, ROWS, WIDTH), BF16),
            pltpu.VMEM((PIECES, len(RETURN), GROUP, ROWS, WIDTH), BF16),
            pltpu.VMEM((PIECES, len(RETURN), GROUP, ROWS, WIDTH), BF16),
            pltpu.VMEM((4, 16, 512), BF16),
            pltpu.VMEM((4, 16, 512), BF16),
            pltpu.VMEM((4, 16, 512), BF16),
            pltpu.VMEM((GROUP, ROWS, PIECES * WIDTH), BF16),
            pltpu.VMEM((GROUP, ROWS, QUARTER), BF16),
            pltpu.VMEM((GROUP, ROWS, QUARTER), BF16),
            dma((5,)), dma((REQ,)), dma((3,)), dma((3,)), dma((7,)), dma((7,)),
            dma((PIECES, len(PLAN))), dma((PIECES, len(PLAN))),
            dma((PIECES, 8)), dma((PIECES, 8)),
            dma((PIECES, 2)), dma((PIECES, 2)),
            dma((PIECES, len(RETURN))), dma((PIECES, len(RETURN))), dma((7,)), dma((7,)),
            dma((3,)), dma((3,)),
        ],
        compiler_params=pltpu.CompilerParams(
            collective_id=0, has_side_effects=True, vmem_limit_bytes=60 * 1024 * 1024),
    )(tokens, routes, gates, lengths, w_gate, w_up, w_down,
      queries.transpose(0, 2, 1), cache.transpose(0, 2, 1))
    return pl.pallas_call(
        finish,
        out_shape=(
            jax.ShapeDtypeStruct((REQ, D), BF16),
            jax.ShapeDtypeStruct((REQ, HEADS, LATENT), BF16),
        ),
        in_specs=[vmem, vmem],
        out_specs=(vmem, vmem),
    )(got, att)


def solution(mesh):
    a = ("side", "dev")
    in_specs = (P(a, None),) * 3 + (P(a, None, None),) * 5 + (P(a),)
    out_specs = (P(a, None), P(a, None, None))
    return jax.shard_map(
        per_device, mesh=mesh, in_specs=in_specs, out_specs=out_specs, check_vma=False
    )
```

```python
import jax
import jax.numpy as jnp
from jax import lax
from jax.experimental import pallas as pl
from jax.experimental.pallas import tpu as pltpu
from jax.sharding import PartitionSpec as P

D = 7168
UNITS = 256
LATENT = 512
KEY = 576
HEADS = 128
MAX_LEN = 1024
REQ = 4
EXPERTS = 16
SCALE = 192.0 ** -0.5

QUARTER = 1792
PIECES = 3
NEAR_FIRST = ((2, 0), (1, 0), (3, 0), (2, 1), (1, 1), (3, 1), (0, 1))
UNROLL = True
WIDTH = 640
USED = (640, 640, 512)
ROWS = 16
BLOCKS = 64
GROUP = 8
MESH = pl.DeviceIdType.MESH
F32 = jnp.float32
BF16 = jnp.bfloat16


PLAN = ((3, 0, 0), (3, 0, 1), (4, 0, 0), (4, 0, 1), (5, 0, 0), (4, 1, None), (5, 1, None),
        (5, 2, None), (5, 3, None), (5, 0, 1))
NEAR = {3: 1, 4: 2, 5: 4}
RETURN = ((5, 4), (5, 5), (5, 6), (5, 7), (4, 2), (4, 3), (3, 1))


def bit_of(c, beta):
    if isinstance(c, int):
        high, low = c // 2, ((c + 1) // 2) % 2
    else:
        high, low = lax.div(c, 2), lax.rem(lax.div(c + 1, 2), 2)
    return beta * high + (1 - beta) * low


def flip_of(c, beta):
    return beta * (3 - c) + (1 - beta) * (c + 1 - 2 * lax.rem(c, 2))


def row_part(p, s, yy, ww):
    high = (bit_of(ww, 0) * (1 << (0 - p) % 3) + bit_of(yy, 1 - s) * (1 << (1 - p) % 3)
            + bit_of(ww, 1) * (1 << (2 - p) % 3))
    return 4 * bit_of(yy, s) + GROUP * high


def flip_bits(n, mask):
    out = n
    for k in range(3):
        if mask >> k & 1:
            out = out + (1 << k) * (1 - 2 * lax.rem(lax.div(n, 1 << k), 2))
    return out


def kernel(
    tokens, routes, gates, lengths, w_gate, w_up, w_down, queries, cache,
    got2, att_out,
    x_buf, wg, wu, wd, kv, qs, att, acc, hid, gexp, total, sib_out, sib_in, out_buf, in_buf,
    pack, got, cube, cube_out, cube_in,
    local_sem, att_sem, cube_send, cube_recv, ag_send, ag_recv, sib_send, sib_recv,
    rsib_send, rsib_recv, rs_send, rs_recv, back_send, back_recv,
):
    s = lax.axis_index("side")
    dev = lax.axis_index("dev")
    x, y, z = lax.rem(dev, 4), lax.rem(lax.div(dev, 4), 4), lax.div(dev, 16)
    t = 1 - s
    r, w_at = (1 - s) * x + s * z, (1 - s) * z + s * x

    def chip(cr, cy, cw):
        return (s, (1 - s) * (cw * 16 + cy * 4 + cr) + s * (cr * 16 + cy * 4 + cw))

    def cube_peer(d, f):
        return chip(lax.rem(r + d, 4), flip_of(y, s) if f else y, w_at)

    def partner(p, k):
        a = (k + p) % 3
        if a == 1:
            return chip(r, flip_of(y, 1 - s), w_at)
        return chip(r, y, flip_of(w_at, 0 if a == 0 else 1))

    sibling = (t, dev)

    loads = [
        pltpu.make_async_copy(queries, qs, local_sem.at[0]),
        pltpu.make_async_copy(cache, kv, local_sem.at[1]),
        pltpu.make_async_copy(w_gate.at[0], wg, local_sem.at[2]),
        pltpu.make_async_copy(w_up.at[0], wu, local_sem.at[3]),
        pltpu.make_async_copy(w_down.at[0], wd, local_sem.at[4]),
    ]

    barrier = pltpu.get_barrier_semaphore()
    greet = [sibling] + [cube_peer(d, f) for f in (0, 1) for d in range(4) if d or f]
    greet += [partner(p, 3) for p in range(PIECES)]
    for who in greet:
        pl.semaphore_signal(barrier, inc=1, device_id=who, device_id_type=MESH)
    for load in loads:
        load.start()

    lane = lax.broadcasted_iota(jnp.int32, (4, 128), 1)
    dense = jnp.zeros((4, 128), F32)
    for k in range(8):
        dense += jnp.where(routes[:, k:k + 1] == (lane & 15), gates[:, k:k + 1], 0.0)
    first = dense.astype(BF16).astype(F32)
    second = (dense - first).astype(BF16).astype(F32)
    third = dense - first - second
    aux = jnp.where(lane < 16, first, jnp.where(lane < 32, second, jnp.where(lane < 48, third, 0.0)))
    aux = jnp.concatenate([aux, jnp.zeros((4, 128), F32)], 1)
    for j in range(4):
        parts = []
        for c in range(4):
            lo = QUARTER * j + 512 * c
            if c < 3:
                parts.append(tokens[:, lo:lo + 512].astype(F32))
            else:
                parts.append(jnp.concatenate([tokens[:, lo:lo + 256].astype(F32), aux], 1))
        pack[j] = jnp.concatenate(parts, 0).astype(BF16)

    pl.semaphore_wait(barrier, len(greet))

    own = [r + row_part(p, s, y, w_at) for p in range(PIECES)]
    theirs = [w_at + row_part(p, t, y, r) for p in range(PIECES)]
    low = lax.rem(own[0], GROUP)
    high = [lax.div(n, GROUP) for n in own]
    high_theirs = [lax.div(n, GROUP) for n in theirs]

    def place_of(d, f):
        mine = lax.div(low, 4)
        return lax.rem(r + d, 4) + 4 * (1 - mine if f else mine)

    def cube_copy(d, f):
        return pltpu.make_async_remote_copy(
            src_ref=pack, dst_ref=got.at[low],
            send_sem=cube_send.at[d + 4 * f], recv_sem=cube_recv.at[d + 4 * f],
            device_id=cube_peer(d, f), device_id_type=MESH)

    def cube_arrival(d, f):
        return pltpu.make_async_remote_copy(
            src_ref=pack, dst_ref=got.at[place_of(4 - d, f)],
            send_sem=cube_send.at[d + 4 * f], recv_sem=cube_recv.at[d + 4 * f],
            device_id=cube_peer(d, f), device_id_type=MESH)

    def half_start(h):
        mine = lax.div(low, 4)
        return 4 * (mine if h == 0 else 1 - mine)

    row = lax.broadcasted_iota(jnp.int32, (64, 64), 0)
    col = lax.broadcasted_iota(jnp.int32, (64, 64), 1)
    swap = ((row >> 4) == ((col >> 2) & 3)) & (((row >> 2) & 3) == (col >> 4)) & ((row & 3) == (col & 3))
    swap = jnp.where(swap, 1.0, 0.0).astype(BF16)

    def assemble(h):
        begin = half_start(h)
        for j in range(4):
            rows = got[pl.ds(begin, 4), j].reshape(64, 512)
            turned = jnp.dot(swap, rows, preferred_element_type=F32).astype(BF16)
            for c in range(4):
                wide = 512 if c < 3 else 384
                cube[begin + j, :, 512 * c:512 * c + wide] = turned[16 * c:16 * (c + 1), :wide]

    def ag_copy(p, i):
        k, unit, h = PLAN[i]
        begin, size = (0, 8) if h is None else (half_start(h), 4)
        dst = x_buf.at[s, p, pl.ds(flip_bits(high[p], unit) * GROUP + begin, size)]
        if unit == 0:
            src = cube.at[pl.ds(begin, size), :, pl.ds(p * WIDTH, WIDTH)]
        else:
            src = dst
        return pltpu.make_async_remote_copy(
            src_ref=src, dst_ref=dst, send_sem=ag_send.at[p, i], recv_sem=ag_recv.at[p, i],
            device_id=partner(p, k), device_id_type=MESH)

    def ag_arrival(p, i):
        k, unit, h = PLAN[i]
        begin, size = (0, 8) if h is None else (4 * h, 4)
        came = x_buf.at[s, p, pl.ds(flip_bits(high[p], unit ^ NEAR[k]) * GROUP + begin, size)]
        return pltpu.make_async_remote_copy(
            src_ref=came, dst_ref=came, send_sem=ag_send.at[p, i], recv_sem=ag_recv.at[p, i],
            device_id=partner(p, k), device_id_type=MESH)

    def forward(p, unit, top, side):
        region = x_buf.at[side, p, pl.ds(flip_bits(top, unit) * GROUP, GROUP)]
        return pltpu.make_async_remote_copy(
            src_ref=region, dst_ref=region, send_sem=sib_send.at[p, unit], recv_sem=sib_recv.at[p, unit],
            device_id=sibling, device_id_type=MESH)

    def attend(r):
        scores = jnp.dot(qs[r].T, kv[r], preferred_element_type=F32) * SCALE
        valid = lax.broadcasted_iota(jnp.int32, (HEADS, MAX_LEN), 1) < lengths[r]
        scores = jnp.where(valid, scores, -1e30)
        highest = jnp.max(scores, -1, keepdims=True)
        weights = jnp.where(valid, jnp.exp(scores - highest), 0.0)
        chance = (weights / jnp.sum(weights, -1, keepdims=True)).astype(BF16)
        att[r] = lax.dot_general(
            chance, kv[r, :LATENT, :], (((1,), (1,)), ((), ())), preferred_element_type=F32).astype(BF16)
        pltpu.make_async_copy(att.at[r], att_out.at[r], att_sem.at[r]).start()

    acc[...] = jnp.zeros_like(acc)
    for d, f in NEAR_FIRST:
        cube_copy(d, f).start()
    got[low] = pack[...]
    loads[0].wait()
    loads[1].wait()
    attend(0)
    attend(1)
    for d in (1, 3, 2):
        cube_arrival(d, 0).wait_recv()
    assemble(0)
    for i in (0, 2, 4):
        for p in range(PIECES):
            ag_copy(p, i).start()
    attend(2)
    for d in (0, 1, 3, 2):
        cube_arrival(d, 1).wait_recv()
    assemble(1)
    for i in (1, 3, 9):
        for p in range(PIECES):
            ag_copy(p, i).start()
    for p in range(PIECES):
        x_buf[s, p, pl.ds(high[p] * GROUP, GROUP)] = cube[:, :, WIDTH * p:WIDTH * (p + 1)]
    for p in range(PIECES):
        forward(p, 0, high[p], s).start()
    attend(3)
    for arrived, unit, sent in (((0, 1), 1, (5, 6)), ((2, 3), 2, (7,)), ((5,), 3, (8,))):
        for p in range(PIECES):
            for i in arrived:
                ag_arrival(p, i).wait_recv()
            for i in sent:
                ag_copy(p, i).start()
            forward(p, unit, high[p], s).start()

    def half_rows(side, p, b):
        every = (0, 1, 2, 3)
        if p == 0:
            return (2 * b, 2 * b + 1), every
        if p == 1:
            return (b, 3 - b), every
        beta = 1 - side
        return every, (beta * 2 * b + (1 - beta) * b, beta * (2 * b + 1) + (1 - beta) * (3 - b))

    def project(side, p, b):
        w = USED[p]
        zs, ys = half_rows(side, p, b)

        def step(q, carry):
            tiles = [
                x_buf[side, p, q + row_part(p, side, yy, zz), :, :w]
                for zz in zs for yy in ys]
            lhs = jnp.concatenate(tiles, 0)
            deep = pl.ds(pl.multiple_of(q * QUARTER + p * WIDTH, 128), w)
            for weight, lo in ((wg, 0), (wu, UNITS)):
                res = jnp.dot(lhs, weight[deep, :], preferred_element_type=F32)
                for m, zz in enumerate(zs):
                    for n, yy in enumerate(ys):
                        at = (m * len(ys) + n) * ROWS
                        acc[side, zz * 4 + yy, :, lo:lo + UNITS] += res[at:at + ROWS]
            return carry

        lax.fori_loop(0, 4, step, 0, unroll=UNROLL)

    def bit5(p, side):
        if p == 2:
            return bit_of(y, 1 - side)
        other = (1 - side) * z + side * x
        return bit_of(other, 1 - p)

    loads[2].wait()
    loads[3].wait()
    for p in range(PIECES):
        project(s, p, bit5(p, s))
    for p in range(PIECES):
        for unit in range(4):
            forward(p, unit, high_theirs[p], t).wait_recv()
        project(t, p, bit5(p, t))
    for unit, arrived in ((4, (4, 9)), (5, (6,)), (6, (7,)), (7, (8,))):
        for p in range(PIECES):
            for i in arrived:
                ag_arrival(p, i).wait_recv()
            forward(p, unit, high[p], s).start()
    for p in range(PIECES):
        project(s, p, 1 - bit5(p, s))
    for p in range(PIECES):
        for unit in range(4, 8):
            forward(p, unit, high_theirs[p], t).wait_recv()
        project(t, p, 1 - bit5(p, t))

    expert = s * 8 + z * 2 + lax.div(y, 2)
    deep_lane = lax.broadcasted_iota(jnp.int32, (128, 128), 0)
    select = jnp.where(((deep_lane & 15) == expert) & (deep_lane < 48), 1.0, 0.0).astype(BF16)
    for side in (t, s):
        both = acc[side].reshape(256, 2 * UNITS)
        gate, upper = both[:, :UNITS], both[:, UNITS:]
        hid[side] = (gate / (1.0 + jnp.exp(-gate)) * upper).astype(BF16).reshape(16, ROWS, UNITS)
        tiles = [
            x_buf[side, 2, row_part(2, side, yy, zz), :, 512:640]
            for zz in range(4) for yy in range(4)]
        gexp[side] = jnp.dot(
            jnp.concatenate(tiles, 0), select, preferred_element_type=F32).reshape(16, ROWS, 128)
    loads[4].wait()

    def down(side, p, b, put):
        w = USED[p]
        zs, ys = half_rows(side, p, b)
        lhs = jnp.concatenate([hid[side, zz * 4 + yy] for zz in zs for yy in ys], 0)
        share = jnp.concatenate([gexp[side, zz * 4 + yy] for zz in zs for yy in ys], 0)
        share = jnp.concatenate([share] * (w // 128), 1)

        def step(q, carry):
            wide = pl.ds(pl.multiple_of(q * QUARTER + p * WIDTH, 128), w)
            res = jnp.dot(lhs, wd[:, wide], preferred_element_type=F32) * share
            for m, zz in enumerate(zs):
                for n, yy in enumerate(ys):
                    at = (m * len(ys) + n) * ROWS
                    put(q + row_part(p, side, yy, zz), res[at:at + ROWS])
            return carry

        lax.fori_loop(0, 4, step, 0, unroll=UNROLL)

    def half_copy(p, h, n):
        b = lax.div(n, 32)
        begin = (1 - b) * 32 if h == 0 else b * 32
        w = USED[p]
        return pltpu.make_async_remote_copy(
            src_ref=sib_out.at[p, pl.ds(begin, 32), :, pl.ds(0, w)],
            dst_ref=sib_in.at[p, pl.ds(begin, 32), :, pl.ds(0, w)],
            send_sem=rsib_send.at[p, h], recv_sem=rsib_recv.at[p, h],
            device_id=sibling, device_id_type=MESH)

    def rs_copy(p, i):
        w = USED[p]
        return pltpu.make_async_remote_copy(
            src_ref=out_buf.at[p, i, :, :, pl.ds(0, w)], dst_ref=in_buf.at[p, i, :, :, pl.ds(0, w)],
            send_sem=rs_send.at[p, i], recv_sem=rs_recv.at[p, i],
            device_id=partner(p, RETURN[i][0]), device_id_type=MESH)

    def came_for(unit):
        return [] if unit > 3 else [unit] + ([4 + unit] if unit < 2 else []) + ([6] if unit < 1 else [])

    def summed(p, unit, j):
        w = USED[p]
        n = flip_bits(high[p], unit) * GROUP + j
        value = total[p, n, :, :w] + sib_in[p, n, :, :w].astype(F32)
        for slot in came_for(unit):
            value += in_buf[p, slot, j, :, :w].astype(F32)
        return value

    def give(p, i):
        def step(j, carry):
            out_buf[p, i, j, :, :USED[p]] = summed(p, RETURN[i][1], j).astype(BF16)
            return carry

        lax.fori_loop(0, GROUP, step, 0)
        rs_copy(p, i).start()

    def put_out(p):
        def put(n, val):
            sib_out[p, n, :, :USED[p]] = val.astype(BF16)
        return put

    def put_total(p):
        def put(n, val):
            total[p, n, :, :USED[p]] = val
        return put

    for p in range(PIECES):
        down(t, p, 1 - bit5(p, t), put_out(p))
        half_copy(p, 0, theirs[p]).start()
    for p in range(PIECES):
        down(s, p, 1 - bit5(p, s), put_total(p))
        half_copy(p, 0, own[p]).wait_recv()
        for i in (3, 2, 1, 0):
            give(p, i)
    for p in range(PIECES):
        down(t, p, bit5(p, t), put_out(p))
        half_copy(p, 1, theirs[p]).start()
    for p in range(PIECES):
        down(s, p, bit5(p, s), put_total(p))
        half_copy(p, 1, own[p]).wait_recv()
    for i, before in ((5, (3,)), (4, (2,)), (6, (1, 5))):
        for p in range(PIECES):
            for slot in before:
                rs_copy(p, slot).wait_recv()
            give(p, i)
    for p in range(PIECES):
        for slot in (0, 4, 6):
            rs_copy(p, slot).wait_recv()

    def back_copy(d, f):
        return pltpu.make_async_remote_copy(
            src_ref=cube_out.at[place_of(d, f)], dst_ref=cube_in.at[low],
            send_sem=back_send.at[d + 4 * f], recv_sem=back_recv.at[d + 4 * f],
            device_id=cube_peer(d, f), device_id_type=MESH)

    def back_arrival(d, f):
        came = cube_in.at[place_of(4 - d, f)]
        return pltpu.make_async_remote_copy(
            src_ref=came, dst_ref=came,
            send_sem=back_send.at[d + 4 * f], recv_sem=back_recv.at[d + 4 * f],
            device_id=cube_peer(d, f), device_id_type=MESH)

    def part_out(h):
        begin = half_start(h)
        for j in range(4):
            whole = jnp.concatenate(
                [summed(p, 0, begin + j).astype(BF16) for p in range(PIECES)] + [jnp.zeros((ROWS, 256), BF16)], 1)
            stacked = jnp.concatenate([whole[:, 512 * c:512 * (c + 1)] for c in range(4)], 0)
            turned = jnp.dot(swap, stacked, preferred_element_type=F32).astype(BF16)
            cube_out[pl.ds(begin, 4), j] = turned.reshape(4, ROWS, 512)

    part_out(1)
    for d in (2, 1, 3, 0):
        back_copy(d, 1).start()
    part_out(0)
    for d in (2, 1, 3):
        back_copy(d, 0).start()
    result = cube_out[low].astype(F32)
    for d, f in ((1, 0), (3, 0), (0, 1), (2, 0), (1, 1), (3, 1), (2, 1)):
        back_arrival(d, f).wait_recv()
        result += cube_in[place_of(4 - d, f)].astype(F32)
    got2[...] = result.astype(BF16)

    for d, f in NEAR_FIRST:
        cube_copy(d, f).wait_send()
        back_copy(d, f).wait_send()
    for p in range(PIECES):
        for i in range(len(PLAN)):
            ag_copy(p, i).wait_send()
        for unit in range(8):
            forward(p, unit, high[p], s).wait_send()
        for h in range(2):
            half_copy(p, h, theirs[p]).wait_send()
        for i in range(len(RETURN)):
            rs_copy(p, i).wait_send()
    for r in range(REQ):
        pltpu.make_async_copy(att.at[r], att_out.at[r], att_sem.at[r]).wait()


def finish(got, att, moe_out, att_out):
    att_out[...] = att[...]
    row = lax.broadcasted_iota(jnp.int32, (8, 16), 0)
    col = lax.broadcasted_iota(jnp.int32, (8, 16), 1)
    for j in range(4):
        for c in range(4):
            hit = (row < 4) & (col == c * 4 + row)
            value = jnp.dot(jnp.where(hit, 1.0, 0.0).astype(BF16), got[j], preferred_element_type=F32)
            w = 512 if c < 3 else 256
            lo = QUARTER * j + 512 * c
            moe_out[:, lo:lo + w] = value[:4, :w].astype(BF16)


def per_device(tokens, routes, gates, w_gate, w_up, w_down, queries, cache, lengths):
    vmem = pl.BlockSpec(memory_space=pltpu.VMEM)
    smem = pl.BlockSpec(memory_space=pltpu.SMEM)
    hbm = pl.BlockSpec(memory_space=pl.ANY)
    dma = pltpu.SemaphoreType.DMA
    got, att = pl.pallas_call(
        kernel,
        out_shape=(
            jax.ShapeDtypeStruct((4, 16, 512), BF16),
            jax.ShapeDtypeStruct((REQ, HEADS, LATENT), BF16),
        ),
        in_specs=[vmem, vmem, vmem, smem, hbm, hbm, hbm, hbm, hbm],
        out_specs=(vmem, hbm),
        scratch_shapes=[
            pltpu.VMEM((2, PIECES, BLOCKS, ROWS, WIDTH), BF16),
            pltpu.VMEM((D, UNITS), BF16),
            pltpu.VMEM((D, UNITS), BF16),
            pltpu.VMEM((UNITS, D), BF16),
            pltpu.VMEM((REQ, KEY, MAX_LEN), BF16),
            pltpu.VMEM((REQ, KEY, HEADS), BF16),
            pltpu.VMEM((REQ, HEADS, LATENT), BF16),
            pltpu.VMEM((2, 16, ROWS, 2 * UNITS), F32),
            pltpu.VMEM((2, 16, ROWS, UNITS), BF16),
            pltpu.VMEM((2, 16, ROWS, 128), F32),
            pltpu.VMEM((PIECES, BLOCKS, ROWS, WIDTH), F32),
            pltpu.VMEM((PIECES, BLOCKS, ROWS, WIDTH), BF16),
            pltpu.VMEM((PIECES, BLOCKS, ROWS, WIDTH), BF16),
            pltpu.VMEM((PIECES, len(RETURN), GROUP, ROWS, WIDTH), BF16),
            pltpu.VMEM((PIECES, len(RETURN), GROUP, ROWS, WIDTH), BF16),
            pltpu.VMEM((4, 16, 512), BF16),
            pltpu.VMEM((GROUP, 4, ROWS, 512), BF16),
            pltpu.VMEM((GROUP, ROWS, PIECES * WIDTH), BF16),
            pltpu.VMEM((GROUP, 4, ROWS, 512), BF16),
            pltpu.VMEM((GROUP, 4, ROWS, 512), BF16),
            dma((5,)), dma((REQ,)), dma((8,)), dma((8,)),
            dma((PIECES, len(PLAN))), dma((PIECES, len(PLAN))),
            dma((PIECES, 8)), dma((PIECES, 8)),
            dma((PIECES, 2)), dma((PIECES, 2)),
            dma((PIECES, len(RETURN))), dma((PIECES, len(RETURN))), dma((8,)), dma((8,)),
        ],
        compiler_params=pltpu.CompilerParams(
            collective_id=0, has_side_effects=True, vmem_limit_bytes=60 * 1024 * 1024),
    )(tokens, routes, gates, lengths, w_gate, w_up, w_down,
      queries.transpose(0, 2, 1), cache.transpose(0, 2, 1))
    return pl.pallas_call(
        finish,
        out_shape=(
            jax.ShapeDtypeStruct((REQ, D), BF16),
            jax.ShapeDtypeStruct((REQ, HEADS, LATENT), BF16),
        ),
        in_specs=[vmem, vmem],
        out_specs=(vmem, vmem),
    )(got, att)


def solution(mesh):
    a = ("side", "dev")
    in_specs = (P(a, None),) * 3 + (P(a, None, None),) * 5 + (P(a),)
    out_specs = (P(a, None), P(a, None, None))
    return jax.shard_map(
        per_device, mesh=mesh, in_specs=in_specs, out_specs=out_specs, check_vma=False
    )
```

```python
import jax
import jax.numpy as jnp
from jax import lax
from jax.experimental import pallas as pl
from jax.experimental.pallas import tpu as pltpu
from jax.sharding import PartitionSpec as P

D = 7168
UNITS = 256
LATENT = 512
KEY = 576
HEADS = 128
MAX_LEN = 1024
REQ = 4
EXPERTS = 16
SCALE = 192.0 ** -0.5

QUARTER = 1792
PIECES = 3
NEAR_FIRST = ((2, 0), (1, 0), (3, 0), (2, 1), (1, 1), (3, 1), (0, 1))
UNROLL = True
WIDTH = 640
USED = (640, 640, 512)
ROWS = 16
BLOCKS = 64
GROUP = 8
MESH = pl.DeviceIdType.MESH
F32 = jnp.float32
BF16 = jnp.bfloat16


PLAN = ((3, 0, 0), (3, 0, 1), (4, 0, 0), (4, 0, 1), (5, 0, 0), (4, 1, None), (5, 1, None),
        (5, 2, None), (5, 3, None), (5, 0, 1))
NEAR = {3: 1, 4: 2, 5: 4}
RETURN = ((5, 4), (5, 5), (5, 6), (5, 7), (4, 2), (4, 3), (3, 1))


def bit_of(c, beta):
    if isinstance(c, int):
        high, low = c // 2, ((c + 1) // 2) % 2
    else:
        high, low = lax.div(c, 2), lax.rem(lax.div(c + 1, 2), 2)
    return beta * high + (1 - beta) * low


def flip_of(c, beta):
    return beta * (3 - c) + (1 - beta) * (c + 1 - 2 * lax.rem(c, 2))


def row_part(p, s, yy, ww):
    high = (bit_of(ww, 0) * (1 << (0 - p) % 3) + bit_of(yy, 1 - s) * (1 << (1 - p) % 3)
            + bit_of(ww, 1) * (1 << (2 - p) % 3))
    return 4 * bit_of(yy, s) + GROUP * high


def flip_bits(n, mask):
    out = n
    for k in range(3):
        if mask >> k & 1:
            out = out + (1 << k) * (1 - 2 * lax.rem(lax.div(n, 1 << k), 2))
    return out


def kernel(
    tokens_in, routes_in, gates_in, lengths_in, w_gate, w_up, w_down, queries, cache,
    got2, att_out,
    tokens, routes, gates, lengths, x_buf, wg, wu, wd, kv, qs, att, acc, hid, gexp, total, sib_out, sib_in, out_buf, in_buf,
    pack, got, cube, cube_out, cube_in,
    local_sem, att_sem, cube_send, cube_recv, ag_send, ag_recv, sib_send, sib_recv,
    rsib_send, rsib_recv, rs_send, rs_recv, back_send, back_recv,
):
    s = lax.axis_index("side")
    dev = lax.axis_index("dev")
    x, y, z = lax.rem(dev, 4), lax.rem(lax.div(dev, 4), 4), lax.div(dev, 16)
    t = 1 - s
    r, w_at = (1 - s) * x + s * z, (1 - s) * z + s * x

    def chip(cr, cy, cw):
        return (s, (1 - s) * (cw * 16 + cy * 4 + cr) + s * (cr * 16 + cy * 4 + cw))

    def cube_peer(d, f):
        return chip(lax.rem(r + d, 4), flip_of(y, s) if f else y, w_at)

    def partner(p, k):
        a = (k + p) % 3
        if a == 1:
            return chip(r, flip_of(y, 1 - s), w_at)
        return chip(r, y, flip_of(w_at, 0 if a == 0 else 1))

    sibling = (t, dev)

    loads = [
        pltpu.make_async_copy(queries, qs, local_sem.at[0]),
        pltpu.make_async_copy(cache, kv, local_sem.at[1]),
        pltpu.make_async_copy(w_gate.at[0], wg, local_sem.at[2]),
        pltpu.make_async_copy(w_up.at[0], wu, local_sem.at[3]),
        pltpu.make_async_copy(w_down.at[0], wd, local_sem.at[4]),
    ]
    small = [
        pltpu.make_async_copy(tokens_in, tokens, local_sem.at[5]),
        pltpu.make_async_copy(routes_in, routes, local_sem.at[6]),
        pltpu.make_async_copy(gates_in, gates, local_sem.at[7]),
        pltpu.make_async_copy(lengths_in, lengths, local_sem.at[8]),
    ]

    barrier = pltpu.get_barrier_semaphore()
    greet = [sibling] + [cube_peer(d, f) for f in (0, 1) for d in range(4) if d or f]
    greet += [partner(p, 3) for p in range(PIECES)]
    for who in greet:
        pl.semaphore_signal(barrier, inc=1, device_id=who, device_id_type=MESH)
    for load in small + loads:
        load.start()
    for load in small:
        load.wait()

    lane = lax.broadcasted_iota(jnp.int32, (4, 128), 1)
    dense = jnp.zeros((4, 128), F32)
    for k in range(8):
        dense += jnp.where(routes[:, k:k + 1] == (lane & 15), gates[:, k:k + 1], 0.0)
    first = dense.astype(BF16).astype(F32)
    second = (dense - first).astype(BF16).astype(F32)
    third = dense - first - second
    aux = jnp.where(lane < 16, first, jnp.where(lane < 32, second, jnp.where(lane < 48, third, 0.0)))
    aux = jnp.concatenate([aux, jnp.zeros((4, 128), F32)], 1)
    for j in range(4):
        parts = []
        for c in range(4):
            lo = QUARTER * j + 512 * c
            if c < 3:
                parts.append(tokens[:, lo:lo + 512].astype(F32))
            else:
                parts.append(jnp.concatenate([tokens[:, lo:lo + 256].astype(F32), aux], 1))
        pack[j] = jnp.concatenate(parts, 0).astype(BF16)

    pl.semaphore_wait(barrier, len(greet))

    own = [r + row_part(p, s, y, w_at) for p in range(PIECES)]
    theirs = [w_at + row_part(p, t, y, r) for p in range(PIECES)]
    low = lax.rem(own[0], GROUP)
    high = [lax.div(n, GROUP) for n in own]
    high_theirs = [lax.div(n, GROUP) for n in theirs]

    def place_of(d, f):
        mine = lax.div(low, 4)
        return lax.rem(r + d, 4) + 4 * (1 - mine if f else mine)

    def cube_copy(d, f):
        return pltpu.make_async_remote_copy(
            src_ref=pack, dst_ref=got.at[low],
            send_sem=cube_send.at[d + 4 * f], recv_sem=cube_recv.at[d + 4 * f],
            device_id=cube_peer(d, f), device_id_type=MESH)

    def cube_arrival(d, f):
        return pltpu.make_async_remote_copy(
            src_ref=pack, dst_ref=got.at[place_of(4 - d, f)],
            send_sem=cube_send.at[d + 4 * f], recv_sem=cube_recv.at[d + 4 * f],
            device_id=cube_peer(d, f), device_id_type=MESH)

    def half_start(h):
        mine = lax.div(low, 4)
        return 4 * (mine if h == 0 else 1 - mine)

    row = lax.broadcasted_iota(jnp.int32, (64, 64), 0)
    col = lax.broadcasted_iota(jnp.int32, (64, 64), 1)
    swap = ((row >> 4) == ((col >> 2) & 3)) & (((row >> 2) & 3) == (col >> 4)) & ((row & 3) == (col & 3))
    swap = jnp.where(swap, 1.0, 0.0).astype(BF16)

    def assemble(h):
        begin = half_start(h)
        for j in range(4):
            rows = got[pl.ds(begin, 4), j].reshape(64, 512)
            turned = jnp.dot(swap, rows, preferred_element_type=F32).astype(BF16)
            for c in range(4):
                wide = 512 if c < 3 else 384
                cube[begin + j, :, 512 * c:512 * c + wide] = turned[16 * c:16 * (c + 1), :wide]

    def ag_copy(p, i):
        k, unit, h = PLAN[i]
        begin, size = (0, 8) if h is None else (half_start(h), 4)
        dst = x_buf.at[s, p, pl.ds(flip_bits(high[p], unit) * GROUP + begin, size)]
        if unit == 0:
            src = cube.at[pl.ds(begin, size), :, pl.ds(p * WIDTH, WIDTH)]
        else:
            src = dst
        return pltpu.make_async_remote_copy(
            src_ref=src, dst_ref=dst, send_sem=ag_send.at[p, i], recv_sem=ag_recv.at[p, i],
            device_id=partner(p, k), device_id_type=MESH)

    def ag_arrival(p, i):
        k, unit, h = PLAN[i]
        begin, size = (0, 8) if h is None else (4 * h, 4)
        came = x_buf.at[s, p, pl.ds(flip_bits(high[p], unit ^ NEAR[k]) * GROUP + begin, size)]
        return pltpu.make_async_remote_copy(
            src_ref=came, dst_ref=came, send_sem=ag_send.at[p, i], recv_sem=ag_recv.at[p, i],
            device_id=partner(p, k), device_id_type=MESH)

    def forward(p, unit, top, side):
        region = x_buf.at[side, p, pl.ds(flip_bits(top, unit) * GROUP, GROUP)]
        return pltpu.make_async_remote_copy(
            src_ref=region, dst_ref=region, send_sem=sib_send.at[p, unit], recv_sem=sib_recv.at[p, unit],
            device_id=sibling, device_id_type=MESH)

    def attend(r):
        scores = jnp.dot(qs[r].T, kv[r], preferred_element_type=F32) * SCALE
        valid = lax.broadcasted_iota(jnp.int32, (HEADS, MAX_LEN), 1) < lengths[r]
        scores = jnp.where(valid, scores, -1e30)
        highest = jnp.max(scores, -1, keepdims=True)
        weights = jnp.where(valid, jnp.exp(scores - highest), 0.0)
        chance = (weights / jnp.sum(weights, -1, keepdims=True)).astype(BF16)
        att[r] = lax.dot_general(
            chance, kv[r, :LATENT, :], (((1,), (1,)), ((), ())), preferred_element_type=F32).astype(BF16)
        pltpu.make_async_copy(att.at[r], att_out.at[r], att_sem.at[r]).start()

    acc[...] = jnp.zeros_like(acc)
    for d, f in NEAR_FIRST:
        cube_copy(d, f).start()
    got[low] = pack[...]
    loads[0].wait()
    loads[1].wait()
    attend(0)
    attend(1)
    for d in (1, 3, 2):
        cube_arrival(d, 0).wait_recv()
    assemble(0)
    for i in (0, 2, 4):
        for p in range(PIECES):
            ag_copy(p, i).start()
    attend(2)
    for d in (0, 1, 3, 2):
        cube_arrival(d, 1).wait_recv()
    assemble(1)
    for i in (1, 3, 9):
        for p in range(PIECES):
            ag_copy(p, i).start()
    for p in range(PIECES):
        x_buf[s, p, pl.ds(high[p] * GROUP, GROUP)] = cube[:, :, WIDTH * p:WIDTH * (p + 1)]
    for p in range(PIECES):
        forward(p, 0, high[p], s).start()
    attend(3)
    for arrived, unit, sent in (((0, 1), 1, (5, 6)), ((2, 3), 2, (7,)), ((5,), 3, (8,))):
        for p in range(PIECES):
            for i in arrived:
                ag_arrival(p, i).wait_recv()
            for i in sent:
                ag_copy(p, i).start()
            forward(p, unit, high[p], s).start()

    def half_rows(side, p, b):
        every = (0, 1, 2, 3)
        if p == 0:
            return (2 * b, 2 * b + 1), every
        if p == 1:
            return (b, 3 - b), every
        beta = 1 - side
        return every, (beta * 2 * b + (1 - beta) * b, beta * (2 * b + 1) + (1 - beta) * (3 - b))

    def project(side, p, b):
        w = USED[p]
        zs, ys = half_rows(side, p, b)

        def step(q, carry):
            tiles = [
                x_buf[side, p, q + row_part(p, side, yy, zz), :, :w]
                for zz in zs for yy in ys]
            lhs = jnp.concatenate(tiles, 0)
            deep = pl.ds(pl.multiple_of(q * QUARTER + p * WIDTH, 128), w)
            for weight, lo in ((wg, 0), (wu, UNITS)):
                res = jnp.dot(lhs, weight[deep, :], preferred_element_type=F32)
                for m, zz in enumerate(zs):
                    for n, yy in enumerate(ys):
                        at = (m * len(ys) + n) * ROWS
                        acc[side, zz * 4 + yy, :, lo:lo + UNITS] += res[at:at + ROWS]
            return carry

        lax.fori_loop(0, 4, step, 0, unroll=UNROLL)

    def bit5(p, side):
        if p == 2:
            return bit_of(y, 1 - side)
        other = (1 - side) * z + side * x
        return bit_of(other, 1 - p)

    loads[2].wait()
    loads[3].wait()
    for p in range(PIECES):
        project(s, p, bit5(p, s))
    for p in range(PIECES):
        for unit in range(4):
            forward(p, unit, high_theirs[p], t).wait_recv()
        project(t, p, bit5(p, t))
    for unit, arrived in ((4, (4, 9)), (5, (6,)), (6, (7,)), (7, (8,))):
        for p in range(PIECES):
            for i in arrived:
                ag_arrival(p, i).wait_recv()
            forward(p, unit, high[p], s).start()
    for p in range(PIECES):
        project(s, p, 1 - bit5(p, s))
    for p in range(PIECES):
        for unit in range(4, 8):
            forward(p, unit, high_theirs[p], t).wait_recv()
        project(t, p, 1 - bit5(p, t))

    expert = s * 8 + z * 2 + lax.div(y, 2)
    deep_lane = lax.broadcasted_iota(jnp.int32, (128, 128), 0)
    select = jnp.where(((deep_lane & 15) == expert) & (deep_lane < 48), 1.0, 0.0).astype(BF16)
    for side in (t, s):
        both = acc[side].reshape(256, 2 * UNITS)
        gate, upper = both[:, :UNITS], both[:, UNITS:]
        hid[side] = (gate / (1.0 + jnp.exp(-gate)) * upper).astype(BF16).reshape(16, ROWS, UNITS)
        tiles = [
            x_buf[side, 2, row_part(2, side, yy, zz), :, 512:640]
            for zz in range(4) for yy in range(4)]
        gexp[side] = jnp.dot(
            jnp.concatenate(tiles, 0), select, preferred_element_type=F32).reshape(16, ROWS, 128)
    loads[4].wait()

    def down(side, p, b, put):
        w = USED[p]
        zs, ys = half_rows(side, p, b)
        lhs = jnp.concatenate([hid[side, zz * 4 + yy] for zz in zs for yy in ys], 0)
        share = jnp.concatenate([gexp[side, zz * 4 + yy] for zz in zs for yy in ys], 0)
        share = jnp.concatenate([share] * (w // 128), 1)

        def step(q, carry):
            wide = pl.ds(pl.multiple_of(q * QUARTER + p * WIDTH, 128), w)
            res = jnp.dot(lhs, wd[:, wide], preferred_element_type=F32) * share
            for m, zz in enumerate(zs):
                for n, yy in enumerate(ys):
                    at = (m * len(ys) + n) * ROWS
                    put(q + row_part(p, side, yy, zz), res[at:at + ROWS])
            return carry

        lax.fori_loop(0, 4, step, 0, unroll=UNROLL)

    def half_copy(p, h, n):
        b = lax.div(n, 32)
        begin = (1 - b) * 32 if h == 0 else b * 32
        w = USED[p]
        return pltpu.make_async_remote_copy(
            src_ref=sib_out.at[p, pl.ds(begin, 32), :, pl.ds(0, w)],
            dst_ref=sib_in.at[p, pl.ds(begin, 32), :, pl.ds(0, w)],
            send_sem=rsib_send.at[p, h], recv_sem=rsib_recv.at[p, h],
            device_id=sibling, device_id_type=MESH)

    def rs_copy(p, i):
        w = USED[p]
        return pltpu.make_async_remote_copy(
            src_ref=out_buf.at[p, i, :, :, pl.ds(0, w)], dst_ref=in_buf.at[p, i, :, :, pl.ds(0, w)],
            send_sem=rs_send.at[p, i], recv_sem=rs_recv.at[p, i],
            device_id=partner(p, RETURN[i][0]), device_id_type=MESH)

    def came_for(unit):
        return [] if unit > 3 else [unit] + ([4 + unit] if unit < 2 else []) + ([6] if unit < 1 else [])

    def summed(p, unit, j):
        w = USED[p]
        n = flip_bits(high[p], unit) * GROUP + j
        value = total[p, n, :, :w] + sib_in[p, n, :, :w].astype(F32)
        for slot in came_for(unit):
            value += in_buf[p, slot, j, :, :w].astype(F32)
        return value

    def give(p, i):
        def step(j, carry):
            out_buf[p, i, j, :, :USED[p]] = summed(p, RETURN[i][1], j).astype(BF16)
            return carry

        lax.fori_loop(0, GROUP, step, 0)
        rs_copy(p, i).start()

    def put_out(p):
        def put(n, val):
            sib_out[p, n, :, :USED[p]] = val.astype(BF16)
        return put

    def put_total(p):
        def put(n, val):
            total[p, n, :, :USED[p]] = val
        return put

    for p in range(PIECES):
        down(t, p, 1 - bit5(p, t), put_out(p))
        half_copy(p, 0, theirs[p]).start()
    for p in range(PIECES):
        down(s, p, 1 - bit5(p, s), put_total(p))
        half_copy(p, 0, own[p]).wait_recv()
        for i in (3, 2, 1, 0):
            give(p, i)
    for p in range(PIECES):
        down(t, p, bit5(p, t), put_out(p))
        half_copy(p, 1, theirs[p]).start()
    for p in range(PIECES):
        down(s, p, bit5(p, s), put_total(p))
        half_copy(p, 1, own[p]).wait_recv()
    for i, before in ((5, (3,)), (4, (2,)), (6, (1, 5))):
        for p in range(PIECES):
            for slot in before:
                rs_copy(p, slot).wait_recv()
            give(p, i)
    for p in range(PIECES):
        for slot in (0, 4, 6):
            rs_copy(p, slot).wait_recv()

    def back_copy(d, f):
        return pltpu.make_async_remote_copy(
            src_ref=cube_out.at[place_of(d, f)], dst_ref=cube_in.at[low],
            send_sem=back_send.at[d + 4 * f], recv_sem=back_recv.at[d + 4 * f],
            device_id=cube_peer(d, f), device_id_type=MESH)

    def back_arrival(d, f):
        came = cube_in.at[place_of(4 - d, f)]
        return pltpu.make_async_remote_copy(
            src_ref=came, dst_ref=came,
            send_sem=back_send.at[d + 4 * f], recv_sem=back_recv.at[d + 4 * f],
            device_id=cube_peer(d, f), device_id_type=MESH)

    def part_out(h):
        begin = half_start(h)
        for j in range(4):
            whole = jnp.concatenate(
                [summed(p, 0, begin + j).astype(BF16) for p in range(PIECES)] + [jnp.zeros((ROWS, 256), BF16)], 1)
            stacked = jnp.concatenate([whole[:, 512 * c:512 * (c + 1)] for c in range(4)], 0)
            turned = jnp.dot(swap, stacked, preferred_element_type=F32).astype(BF16)
            cube_out[pl.ds(begin, 4), j] = turned.reshape(4, ROWS, 512)

    part_out(1)
    for d in (2, 1, 3, 0):
        back_copy(d, 1).start()
    part_out(0)
    for d in (2, 1, 3):
        back_copy(d, 0).start()
    result = cube_out[low].astype(F32)
    for d, f in ((1, 0), (3, 0), (0, 1), (2, 0), (1, 1), (3, 1), (2, 1)):
        back_arrival(d, f).wait_recv()
        result += cube_in[place_of(4 - d, f)].astype(F32)
    got2[...] = result.astype(BF16)

    for d, f in NEAR_FIRST:
        cube_copy(d, f).wait_send()
        back_copy(d, f).wait_send()
    for p in range(PIECES):
        for i in range(len(PLAN)):
            ag_copy(p, i).wait_send()
        for unit in range(8):
            forward(p, unit, high[p], s).wait_send()
        for h in range(2):
            half_copy(p, h, theirs[p]).wait_send()
        for i in range(len(RETURN)):
            rs_copy(p, i).wait_send()
    for r in range(REQ):
        pltpu.make_async_copy(att.at[r], att_out.at[r], att_sem.at[r]).wait()


def finish(got, att, moe_out, att_out):
    att_out[...] = att[...]
    row = lax.broadcasted_iota(jnp.int32, (8, 16), 0)
    col = lax.broadcasted_iota(jnp.int32, (8, 16), 1)
    for j in range(4):
        for c in range(4):
            hit = (row < 4) & (col == c * 4 + row)
            value = jnp.dot(jnp.where(hit, 1.0, 0.0).astype(BF16), got[j], preferred_element_type=F32)
            w = 512 if c < 3 else 256
            lo = QUARTER * j + 512 * c
            moe_out[:, lo:lo + w] = value[:4, :w].astype(BF16)


def per_device(tokens, routes, gates, w_gate, w_up, w_down, queries, cache, lengths):
    vmem = pl.BlockSpec(memory_space=pltpu.VMEM)
    hbm = pl.BlockSpec(memory_space=pl.ANY)
    dma = pltpu.SemaphoreType.DMA
    got, att = pl.pallas_call(
        kernel,
        out_shape=(
            jax.ShapeDtypeStruct((4, 16, 512), BF16),
            jax.ShapeDtypeStruct((REQ, HEADS, LATENT), BF16),
        ),
        in_specs=[hbm] * 9,
        out_specs=(vmem, hbm),
        scratch_shapes=[
            pltpu.VMEM((REQ, D), BF16),
            pltpu.VMEM((REQ, 8), jnp.int32),
            pltpu.VMEM((REQ, 8), F32),
            pltpu.SMEM((REQ,), jnp.int32),
            pltpu.VMEM((2, PIECES, BLOCKS, ROWS, WIDTH), BF16),
            pltpu.VMEM((D, UNITS), BF16),
            pltpu.VMEM((D, UNITS), BF16),
            pltpu.VMEM((UNITS, D), BF16),
            pltpu.VMEM((REQ, KEY, MAX_LEN), BF16),
            pltpu.VMEM((REQ, KEY, HEADS), BF16),
            pltpu.VMEM((REQ, HEADS, LATENT), BF16),
            pltpu.VMEM((2, 16, ROWS, 2 * UNITS), F32),
            pltpu.VMEM((2, 16, ROWS, UNITS), BF16),
            pltpu.VMEM((2, 16, ROWS, 128), F32),
            pltpu.VMEM((PIECES, BLOCKS, ROWS, WIDTH), F32),
            pltpu.VMEM((PIECES, BLOCKS, ROWS, WIDTH), BF16),
            pltpu.VMEM((PIECES, BLOCKS, ROWS, WIDTH), BF16),
            pltpu.VMEM((PIECES, len(RETURN), GROUP, ROWS, WIDTH), BF16),
            pltpu.VMEM((PIECES, len(RETURN), GROUP, ROWS, WIDTH), BF16),
            pltpu.VMEM((4, 16, 512), BF16),
            pltpu.VMEM((GROUP, 4, ROWS, 512), BF16),
            pltpu.VMEM((GROUP, ROWS, PIECES * WIDTH), BF16),
            pltpu.VMEM((GROUP, 4, ROWS, 512), BF16),
            pltpu.VMEM((GROUP, 4, ROWS, 512), BF16),
            dma((9,)), dma((REQ,)), dma((8,)), dma((8,)),
            dma((PIECES, len(PLAN))), dma((PIECES, len(PLAN))),
            dma((PIECES, 8)), dma((PIECES, 8)),
            dma((PIECES, 2)), dma((PIECES, 2)),
            dma((PIECES, len(RETURN))), dma((PIECES, len(RETURN))), dma((8,)), dma((8,)),
        ],
        compiler_params=pltpu.CompilerParams(
            collective_id=0, has_side_effects=True, vmem_limit_bytes=60 * 1024 * 1024),
    )(tokens, routes, gates, lengths, w_gate, w_up, w_down,
      queries.transpose(0, 2, 1), cache.transpose(0, 2, 1))
    return pl.pallas_call(
        finish,
        out_shape=(
            jax.ShapeDtypeStruct((REQ, D), BF16),
            jax.ShapeDtypeStruct((REQ, HEADS, LATENT), BF16),
        ),
        in_specs=[vmem, vmem],
        out_specs=(vmem, vmem),
    )(got, att)


def solution(mesh):
    a = ("side", "dev")
    in_specs = (P(a, None),) * 3 + (P(a, None, None),) * 5 + (P(a),)
    out_specs = (P(a, None), P(a, None, None))
    return jax.shard_map(
        per_device, mesh=mesh, in_specs=in_specs, out_specs=out_specs, check_vma=False
    )
```

```python
import jax
import jax.numpy as jnp
from jax import lax
from jax.experimental import pallas as pl
from jax.experimental.pallas import tpu as pltpu
from jax.sharding import PartitionSpec as P

D = 7168
UNITS = 256
LATENT = 512
KEY = 576
HEADS = 128
MAX_LEN = 1024
REQ = 4
EXPERTS = 16
SCALE = 192.0 ** -0.5

QUARTER = 1792
PIECES = 3
NEAR_FIRST = ((2, 0), (1, 0), (3, 0), (2, 1), (1, 1), (3, 1), (0, 1))
UNROLL = True
WIDTH = 640
USED = (640, 640, 512)
ROWS = 16
BLOCKS = 64
GROUP = 8
MESH = pl.DeviceIdType.MESH
F32 = jnp.float32
BF16 = jnp.bfloat16


PLAN = ((3, 0, 0), (3, 0, 1), (4, 0, 0), (4, 0, 1), (5, 0, 0), (4, 1, None), (5, 1, None),
        (5, 2, None), (5, 3, None), (5, 0, 1))
NEAR = {3: 1, 4: 2, 5: 4}
RETURN = ((5, 4), (5, 5), (5, 6), (5, 7), (4, 2), (4, 3), (3, 1))


def bit_of(c, beta):
    if isinstance(c, int):
        high, low = c // 2, ((c + 1) // 2) % 2
    else:
        high, low = lax.div(c, 2), lax.rem(lax.div(c + 1, 2), 2)
    return beta * high + (1 - beta) * low


def flip_of(c, beta):
    return beta * (3 - c) + (1 - beta) * (c + 1 - 2 * lax.rem(c, 2))


def row_part(p, s, yy, ww):
    high = (bit_of(ww, 0) * (1 << (0 - p) % 3) + bit_of(yy, 1 - s) * (1 << (1 - p) % 3)
            + bit_of(ww, 1) * (1 << (2 - p) % 3))
    return 4 * bit_of(yy, s) + GROUP * high


def flip_bits(n, mask):
    out = n
    for k in range(3):
        if mask >> k & 1:
            out = out + (1 << k) * (1 - 2 * lax.rem(lax.div(n, 1 << k), 2))
    return out


def kernel(
    tokens_in, routes_in, gates_in, lengths_in, w_gate, w_up, w_down, queries, cache,
    got2, att_out,
    tokens, routes, gates, lengths, x_buf, wg, wu, wd, kv, qs, att, acc, hid, gexp, total, sib_out, sib_in, out_buf, in_buf,
    pack, got, cube, cube_out, cube_in,
    local_sem, att_sem, cube_send, cube_recv, ag_send, ag_recv, sib_send, sib_recv,
    rsib_send, rsib_recv, rs_send, rs_recv, back_send, back_recv,
):
    s = lax.axis_index("side")
    dev = lax.axis_index("dev")
    x, y, z = lax.rem(dev, 4), lax.rem(lax.div(dev, 4), 4), lax.div(dev, 16)
    t = 1 - s
    r, w_at = (1 - s) * x + s * z, (1 - s) * z + s * x

    def chip(cr, cy, cw):
        return (s, (1 - s) * (cw * 16 + cy * 4 + cr) + s * (cr * 16 + cy * 4 + cw))

    def cube_peer(d, f):
        return chip(lax.rem(r + d, 4), flip_of(y, s) if f else y, w_at)

    def partner(p, k):
        a = (k + p) % 3
        if a == 1:
            return chip(r, flip_of(y, 1 - s), w_at)
        return chip(r, y, flip_of(w_at, 0 if a == 0 else 1))

    sibling = (t, dev)

    loads = [
        pltpu.make_async_copy(queries, qs, local_sem.at[0]),
        pltpu.make_async_copy(cache, kv, local_sem.at[1]),
        pltpu.make_async_copy(w_gate.at[0], wg, local_sem.at[2]),
        pltpu.make_async_copy(w_up.at[0], wu, local_sem.at[3]),
        pltpu.make_async_copy(w_down.at[0], wd, local_sem.at[4]),
    ]
    small = [
        pltpu.make_async_copy(tokens_in, tokens, local_sem.at[5]),
        pltpu.make_async_copy(routes_in, routes, local_sem.at[6]),
        pltpu.make_async_copy(gates_in, gates, local_sem.at[7]),
        pltpu.make_async_copy(lengths_in, lengths, local_sem.at[8]),
    ]

    barrier = pltpu.get_barrier_semaphore()
    greet = [sibling] + [cube_peer(d, f) for f in (0, 1) for d in range(4) if d or f]
    greet += [partner(p, 3) for p in range(PIECES)]
    for who in greet:
        pl.semaphore_signal(barrier, inc=1, device_id=who, device_id_type=MESH)
    for load in small + loads:
        load.start()
    for load in small:
        load.wait()

    lane = lax.broadcasted_iota(jnp.int32, (4, 128), 1)
    dense = jnp.zeros((4, 128), F32)
    for k in range(8):
        dense += jnp.where(routes[:, k:k + 1] == (lane & 15), gates[:, k:k + 1], 0.0)
    first = dense.astype(BF16).astype(F32)
    second = (dense - first).astype(BF16).astype(F32)
    third = dense - first - second
    aux = jnp.where(lane < 16, first, jnp.where(lane < 32, second, jnp.where(lane < 48, third, 0.0)))
    aux = jnp.concatenate([aux, jnp.zeros((4, 128), F32)], 1)
    for j in range(4):
        parts = []
        for c in range(4):
            lo = QUARTER * j + 512 * c
            if c < 3:
                parts.append(tokens[:, lo:lo + 512].astype(F32))
            else:
                parts.append(jnp.concatenate([tokens[:, lo:lo + 256].astype(F32), aux], 1))
        pack[j] = jnp.concatenate(parts, 0).astype(BF16)

    pl.semaphore_wait(barrier, len(greet))

    own = [r + row_part(p, s, y, w_at) for p in range(PIECES)]
    theirs = [w_at + row_part(p, t, y, r) for p in range(PIECES)]
    low = lax.rem(own[0], GROUP)
    high = [lax.div(n, GROUP) for n in own]
    high_theirs = [lax.div(n, GROUP) for n in theirs]

    def place_of(d, f):
        mine = lax.div(low, 4)
        return lax.rem(r + d, 4) + 4 * (1 - mine if f else mine)

    def cube_copy(d, f):
        return pltpu.make_async_remote_copy(
            src_ref=pack, dst_ref=got.at[low],
            send_sem=cube_send.at[d + 4 * f], recv_sem=cube_recv.at[d + 4 * f],
            device_id=cube_peer(d, f), device_id_type=MESH)

    def cube_arrival(d, f):
        return pltpu.make_async_remote_copy(
            src_ref=pack, dst_ref=got.at[place_of(4 - d, f)],
            send_sem=cube_send.at[d + 4 * f], recv_sem=cube_recv.at[d + 4 * f],
            device_id=cube_peer(d, f), device_id_type=MESH)

    def half_start(h):
        mine = lax.div(low, 4)
        return 4 * (mine if h == 0 else 1 - mine)

    row = lax.broadcasted_iota(jnp.int32, (64, 64), 0)
    col = lax.broadcasted_iota(jnp.int32, (64, 64), 1)
    swap = ((row >> 4) == ((col >> 2) & 3)) & (((row >> 2) & 3) == (col >> 4)) & ((row & 3) == (col & 3))
    swap = jnp.where(swap, 1.0, 0.0).astype(BF16)

    def assemble(h):
        begin = half_start(h)
        for j in range(4):
            rows = got[pl.ds(begin, 4), j].reshape(64, 512)
            turned = jnp.dot(swap, rows, preferred_element_type=F32).astype(BF16)
            for c in range(4):
                wide = 512 if c < 3 else 384
                cube[begin + j, :, 512 * c:512 * c + wide] = turned[16 * c:16 * (c + 1), :wide]

    def ag_copy(p, i):
        k, unit, h = PLAN[i]
        begin, size = (0, 8) if h is None else (half_start(h), 4)
        dst = x_buf.at[s, p, pl.ds(flip_bits(high[p], unit) * GROUP + begin, size)]
        if unit == 0:
            src = cube.at[pl.ds(begin, size), :, pl.ds(p * WIDTH, WIDTH)]
        else:
            src = dst
        return pltpu.make_async_remote_copy(
            src_ref=src, dst_ref=dst, send_sem=ag_send.at[p, i], recv_sem=ag_recv.at[p, i],
            device_id=partner(p, k), device_id_type=MESH)

    def ag_arrival(p, i):
        k, unit, h = PLAN[i]
        begin, size = (0, 8) if h is None else (4 * h, 4)
        came = x_buf.at[s, p, pl.ds(flip_bits(high[p], unit ^ NEAR[k]) * GROUP + begin, size)]
        return pltpu.make_async_remote_copy(
            src_ref=came, dst_ref=came, send_sem=ag_send.at[p, i], recv_sem=ag_recv.at[p, i],
            device_id=partner(p, k), device_id_type=MESH)

    def forward(p, unit, top, side):
        region = x_buf.at[side, p, pl.ds(flip_bits(top, unit) * GROUP, GROUP)]
        return pltpu.make_async_remote_copy(
            src_ref=region, dst_ref=region, send_sem=sib_send.at[p, unit], recv_sem=sib_recv.at[p, unit],
            device_id=sibling, device_id_type=MESH)

    def attend(r):
        scores = jnp.dot(qs[r].T, kv[r], preferred_element_type=F32) * SCALE
        valid = lax.broadcasted_iota(jnp.int32, (HEADS, MAX_LEN), 1) < lengths[r]
        scores = jnp.where(valid, scores, -1e30)
        highest = jnp.max(scores, -1, keepdims=True)
        weights = jnp.where(valid, jnp.exp(scores - highest), 0.0)
        chance = (weights / jnp.sum(weights, -1, keepdims=True)).astype(BF16)
        att[r] = lax.dot_general(
            chance, kv[r, :LATENT, :], (((1,), (1,)), ((), ())), preferred_element_type=F32).astype(BF16)
        pltpu.make_async_copy(att.at[r], att_out.at[r], att_sem.at[r]).start()

    acc[...] = jnp.zeros_like(acc)
    for d, f in NEAR_FIRST:
        cube_copy(d, f).start()
    got[low] = pack[...]
    loads[0].wait()
    loads[1].wait()
    attend(0)
    attend(1)
    for d in (1, 3, 2):
        cube_arrival(d, 0).wait_recv()
    assemble(0)
    for i in (0, 2, 4):
        for p in range(PIECES):
            ag_copy(p, i).start()
    attend(2)
    for d in (0, 1, 3, 2):
        cube_arrival(d, 1).wait_recv()
    assemble(1)
    for i in (1, 3, 9):
        for p in range(PIECES):
            ag_copy(p, i).start()
    for p in range(PIECES):
        x_buf[s, p, pl.ds(high[p] * GROUP, GROUP)] = cube[:, :, WIDTH * p:WIDTH * (p + 1)]
    for p in range(PIECES):
        forward(p, 0, high[p], s).start()
    attend(3)
    for arrived, unit, sent in (((0, 1), 1, (5, 6)), ((2, 3), 2, (7,)), ((5,), 3, (8,))):
        for p in range(PIECES):
            for i in arrived:
                ag_arrival(p, i).wait_recv()
            for i in sent:
                ag_copy(p, i).start()
            forward(p, unit, high[p], s).start()

    def half_rows(side, p, b):
        every = (0, 1, 2, 3)
        if p == 0:
            return (2 * b, 2 * b + 1), every
        if p == 1:
            return (b, 3 - b), every
        beta = 1 - side
        return every, (beta * 2 * b + (1 - beta) * b, beta * (2 * b + 1) + (1 - beta) * (3 - b))

    def project(side, p, b):
        w = USED[p]
        zs, ys = half_rows(side, p, b)

        def step(q, carry):
            tiles = [
                x_buf[side, p, q + row_part(p, side, yy, zz), :, :w]
                for zz in zs for yy in ys]
            lhs = jnp.concatenate(tiles, 0)
            deep = pl.ds(pl.multiple_of(q * QUARTER + p * WIDTH, 128), w)
            for weight, lo in ((wg, 0), (wu, UNITS)):
                res = jnp.dot(lhs, weight[deep, :], preferred_element_type=F32)
                for m, zz in enumerate(zs):
                    for n, yy in enumerate(ys):
                        at = (m * len(ys) + n) * ROWS
                        acc[side, zz * 4 + yy, :, lo:lo + UNITS] += res[at:at + ROWS]
            return carry

        lax.fori_loop(0, 4, step, 0, unroll=UNROLL)

    def bit5(p, side):
        if p == 2:
            return bit_of(y, 1 - side)
        other = (1 - side) * z + side * x
        return bit_of(other, 1 - p)

    loads[2].wait()
    loads[3].wait()
    for p in range(PIECES):
        project(s, p, bit5(p, s))
    for unit, arrived in ((4, (4, 9)),):
        for p in range(PIECES):
            for i in arrived:
                ag_arrival(p, i).wait_recv()
            forward(p, unit, high[p], s).start()
    for p in range(PIECES):
        for unit in range(4):
            forward(p, unit, high_theirs[p], t).wait_recv()
        project(t, p, bit5(p, t))
    for unit, arrived in ((5, (6,)), (6, (7,)), (7, (8,)),):
        for p in range(PIECES):
            for i in arrived:
                ag_arrival(p, i).wait_recv()
            forward(p, unit, high[p], s).start()
    for p in range(PIECES):
        project(s, p, 1 - bit5(p, s))
    for p in range(PIECES):
        for unit in range(4, 8):
            forward(p, unit, high_theirs[p], t).wait_recv()
        project(t, p, 1 - bit5(p, t))

    expert = s * 8 + z * 2 + lax.div(y, 2)
    deep_lane = lax.broadcasted_iota(jnp.int32, (128, 128), 0)
    select = jnp.where(((deep_lane & 15) == expert) & (deep_lane < 48), 1.0, 0.0).astype(BF16)
    for side in (t, s):
        both = acc[side].reshape(256, 2 * UNITS)
        gate, upper = both[:, :UNITS], both[:, UNITS:]
        hid[side] = (gate / (1.0 + jnp.exp(-gate)) * upper).astype(BF16).reshape(16, ROWS, UNITS)
        tiles = [
            x_buf[side, 2, row_part(2, side, yy, zz), :, 512:640]
            for zz in range(4) for yy in range(4)]
        gexp[side] = jnp.dot(
            jnp.concatenate(tiles, 0), select, preferred_element_type=F32).reshape(16, ROWS, 128)
    loads[4].wait()

    def down(side, p, b, put):
        w = USED[p]
        zs, ys = half_rows(side, p, b)
        lhs = jnp.concatenate([hid[side, zz * 4 + yy] for zz in zs for yy in ys], 0)
        share = jnp.concatenate([gexp[side, zz * 4 + yy] for zz in zs for yy in ys], 0)
        share = jnp.concatenate([share] * (w // 128), 1)

        def step(q, carry):
            wide = pl.ds(pl.multiple_of(q * QUARTER + p * WIDTH, 128), w)
            res = jnp.dot(lhs, wd[:, wide], preferred_element_type=F32) * share
            for m, zz in enumerate(zs):
                for n, yy in enumerate(ys):
                    at = (m * len(ys) + n) * ROWS
                    put(q + row_part(p, side, yy, zz), res[at:at + ROWS])
            return carry

        lax.fori_loop(0, 4, step, 0, unroll=UNROLL)

    def half_copy(p, h, n):
        b = lax.div(n, 32)
        begin = (1 - b) * 32 if h == 0 else b * 32
        w = USED[p]
        return pltpu.make_async_remote_copy(
            src_ref=sib_out.at[p, pl.ds(begin, 32), :, pl.ds(0, w)],
            dst_ref=sib_in.at[p, pl.ds(begin, 32), :, pl.ds(0, w)],
            send_sem=rsib_send.at[p, h], recv_sem=rsib_recv.at[p, h],
            device_id=sibling, device_id_type=MESH)

    def rs_copy(p, i):
        w = USED[p]
        return pltpu.make_async_remote_copy(
            src_ref=out_buf.at[p, i, :, :, pl.ds(0, w)], dst_ref=in_buf.at[p, i, :, :, pl.ds(0, w)],
            send_sem=rs_send.at[p, i], recv_sem=rs_recv.at[p, i],
            device_id=partner(p, RETURN[i][0]), device_id_type=MESH)

    def came_for(unit):
        return [] if unit > 3 else [unit] + ([4 + unit] if unit < 2 else []) + ([6] if unit < 1 else [])

    def summed(p, unit, j):
        w = USED[p]
        n = flip_bits(high[p], unit) * GROUP + j
        value = total[p, n, :, :w] + sib_in[p, n, :, :w].astype(F32)
        for slot in came_for(unit):
            value += in_buf[p, slot, j, :, :w].astype(F32)
        return value

    def give(p, i):
        def step(j, carry):
            out_buf[p, i, j, :, :USED[p]] = summed(p, RETURN[i][1], j).astype(BF16)
            return carry

        lax.fori_loop(0, GROUP, step, 0)
        rs_copy(p, i).start()

    def put_out(p):
        def put(n, val):
            sib_out[p, n, :, :USED[p]] = val.astype(BF16)
        return put

    def put_total(p):
        def put(n, val):
            total[p, n, :, :USED[p]] = val
        return put

    for p in range(PIECES):
        down(t, p, 1 - bit5(p, t), put_out(p))
        half_copy(p, 0, theirs[p]).start()
    for p in range(PIECES):
        down(s, p, 1 - bit5(p, s), put_total(p))
        half_copy(p, 0, own[p]).wait_recv()
        for i in (3, 2, 1, 0):
            give(p, i)
    for p in range(PIECES):
        down(t, p, bit5(p, t), put_out(p))
        half_copy(p, 1, theirs[p]).start()
    for p in range(PIECES):
        down(s, p, bit5(p, s), put_total(p))
        half_copy(p, 1, own[p]).wait_recv()
    for i, before in ((5, (3,)), (4, (2,)), (6, (1, 5))):
        for p in range(PIECES):
            for slot in before:
                rs_copy(p, slot).wait_recv()
            give(p, i)
    for p in range(PIECES):
        for slot in (0, 4, 6):
            rs_copy(p, slot).wait_recv()

    def back_copy(d, f):
        return pltpu.make_async_remote_copy(
            src_ref=cube_out.at[place_of(d, f)], dst_ref=cube_in.at[low],
            send_sem=back_send.at[d + 4 * f], recv_sem=back_recv.at[d + 4 * f],
            device_id=cube_peer(d, f), device_id_type=MESH)

    def back_arrival(d, f):
        came = cube_in.at[place_of(4 - d, f)]
        return pltpu.make_async_remote_copy(
            src_ref=came, dst_ref=came,
            send_sem=back_send.at[d + 4 * f], recv_sem=back_recv.at[d + 4 * f],
            device_id=cube_peer(d, f), device_id_type=MESH)

    def part_out(h):
        begin = half_start(h)
        for j in range(4):
            whole = jnp.concatenate(
                [summed(p, 0, begin + j).astype(BF16) for p in range(PIECES)] + [jnp.zeros((ROWS, 256), BF16)], 1)
            stacked = jnp.concatenate([whole[:, 512 * c:512 * (c + 1)] for c in range(4)], 0)
            turned = jnp.dot(swap, stacked, preferred_element_type=F32).astype(BF16)
            cube_out[pl.ds(begin, 4), j] = turned.reshape(4, ROWS, 512)

    part_out(1)
    for d in (2, 1, 3, 0):
        back_copy(d, 1).start()
    part_out(0)
    for d in (2, 1, 3):
        back_copy(d, 0).start()
    result = cube_out[low].astype(F32)
    for d, f in ((1, 0), (3, 0), (0, 1), (2, 0), (1, 1), (3, 1), (2, 1)):
        back_arrival(d, f).wait_recv()
        result += cube_in[place_of(4 - d, f)].astype(F32)
    got2[...] = result.astype(BF16)

    for d, f in NEAR_FIRST:
        cube_copy(d, f).wait_send()
        back_copy(d, f).wait_send()
    for p in range(PIECES):
        for i in range(len(PLAN)):
            ag_copy(p, i).wait_send()
        for unit in range(8):
            forward(p, unit, high[p], s).wait_send()
        for h in range(2):
            half_copy(p, h, theirs[p]).wait_send()
        for i in range(len(RETURN)):
            rs_copy(p, i).wait_send()
    for r in range(REQ):
        pltpu.make_async_copy(att.at[r], att_out.at[r], att_sem.at[r]).wait()


def finish(got, att, moe_out, att_out):
    att_out[...] = att[...]
    row = lax.broadcasted_iota(jnp.int32, (8, 16), 0)
    col = lax.broadcasted_iota(jnp.int32, (8, 16), 1)
    for j in range(4):
        for c in range(4):
            hit = (row < 4) & (col == c * 4 + row)
            value = jnp.dot(jnp.where(hit, 1.0, 0.0).astype(BF16), got[j], preferred_element_type=F32)
            w = 512 if c < 3 else 256
            lo = QUARTER * j + 512 * c
            moe_out[:, lo:lo + w] = value[:4, :w].astype(BF16)


def per_device(tokens, routes, gates, w_gate, w_up, w_down, queries, cache, lengths):
    vmem = pl.BlockSpec(memory_space=pltpu.VMEM)
    hbm = pl.BlockSpec(memory_space=pl.ANY)
    dma = pltpu.SemaphoreType.DMA
    got, att = pl.pallas_call(
        kernel,
        out_shape=(
            jax.ShapeDtypeStruct((4, 16, 512), BF16),
            jax.ShapeDtypeStruct((REQ, HEADS, LATENT), BF16),
        ),
        in_specs=[hbm] * 9,
        out_specs=(vmem, hbm),
        scratch_shapes=[
            pltpu.VMEM((REQ, D), BF16),
            pltpu.VMEM((REQ, 8), jnp.int32),
            pltpu.VMEM((REQ, 8), F32),
            pltpu.SMEM((REQ,), jnp.int32),
            pltpu.VMEM((2, PIECES, BLOCKS, ROWS, WIDTH), BF16),
            pltpu.VMEM((D, UNITS), BF16),
            pltpu.VMEM((D, UNITS), BF16),
            pltpu.VMEM((UNITS, D), BF16),
            pltpu.VMEM((REQ, KEY, MAX_LEN), BF16),
            pltpu.VMEM((REQ, KEY, HEADS), BF16),
            pltpu.VMEM((REQ, HEADS, LATENT), BF16),
            pltpu.VMEM((2, 16, ROWS, 2 * UNITS), F32),
            pltpu.VMEM((2, 16, ROWS, UNITS), BF16),
            pltpu.VMEM((2, 16, ROWS, 128), F32),
            pltpu.VMEM((PIECES, BLOCKS, ROWS, WIDTH), F32),
            pltpu.VMEM((PIECES, BLOCKS, ROWS, WIDTH), BF16),
            pltpu.VMEM((PIECES, BLOCKS, ROWS, WIDTH), BF16),
            pltpu.VMEM((PIECES, len(RETURN), GROUP, ROWS, WIDTH), BF16),
            pltpu.VMEM((PIECES, len(RETURN), GROUP, ROWS, WIDTH), BF16),
            pltpu.VMEM((4, 16, 512), BF16),
            pltpu.VMEM((GROUP, 4, ROWS, 512), BF16),
            pltpu.VMEM((GROUP, ROWS, PIECES * WIDTH), BF16),
            pltpu.VMEM((GROUP, 4, ROWS, 512), BF16),
            pltpu.VMEM((GROUP, 4, ROWS, 512), BF16),
            dma((9,)), dma((REQ,)), dma((8,)), dma((8,)),
            dma((PIECES, len(PLAN))), dma((PIECES, len(PLAN))),
            dma((PIECES, 8)), dma((PIECES, 8)),
            dma((PIECES, 2)), dma((PIECES, 2)),
            dma((PIECES, len(RETURN))), dma((PIECES, len(RETURN))), dma((8,)), dma((8,)),
        ],
        compiler_params=pltpu.CompilerParams(
            collective_id=0, has_side_effects=True, vmem_limit_bytes=60 * 1024 * 1024),
    )(tokens, routes, gates, lengths, w_gate, w_up, w_down,
      queries.transpose(0, 2, 1), cache.transpose(0, 2, 1))
    return pl.pallas_call(
        finish,
        out_shape=(
            jax.ShapeDtypeStruct((REQ, D), BF16),
            jax.ShapeDtypeStruct((REQ, HEADS, LATENT), BF16),
        ),
        in_specs=[vmem, vmem],
        out_specs=(vmem, vmem),
    )(got, att)


def solution(mesh):
    a = ("side", "dev")
    in_specs = (P(a, None),) * 3 + (P(a, None, None),) * 5 + (P(a),)
    out_specs = (P(a, None), P(a, None, None))
    return jax.shard_map(
        per_device, mesh=mesh, in_specs=in_specs, out_specs=out_specs, check_vma=False
    )
```
